128 devices in a mesh: lat: 8 (over z_hi, x), lon: 16 (over z_lo, y, core).
Axes of the slice: x: 4, y: 4, z: 4 (z_hi: 2, z_lo: 2; z = z_hi * 2 + z_lo), core: 2. Of those that a mesh axis runs over, the one named last changes fastest.
Arguments:
- thickness: float32 [32, 2880, 1024], P(None, 'lon', 'lat'), may hold values from 0.5 to 1.5
- tracer_mass: float32 [32, 2880, 1024], P(None, 'lon', 'lat'), may hold values from -6 to 6
- zonal_courant: float32 [32, 2880, 1024], P(None, 'lon', 'lat'), may hold values from -0.45 to 0.45
- merid_courant: float32 [32, 2880, 1024], P(None, 'lon', 'lat'), may hold values from -0.45 to 0.45
- cutoffs: int32 [512], replicated, may hold values from 32 to 256, as said below
Outputs:
- thickness_out: float32 [32, 2880, 1024], P(None, 'lon', 'lat')
- tracer_out: float32 [32, 2880, 1024], P(None, 'lon', 'lat')
The draws below stay inside these ranges and needn't reach their ends.
Inputs may be any that keep to these rules, and one draw needn't show every extreme that they name: Both ends 256 // 8 and 256 occur among the cutoffs.
All inputs are finite; a program needn't handle non-finite values.
Results may differ from the reference program's by a relative error of at most 0.0001.
Values sent between devices are 32-bit elements; how exact they have to be, the bound alone decides.
A program may use at most 256 MiB of HBM per device.

```python
import jax
import jax.numpy as jnp

NLON = 2880
LEV = 32
KW = 256
SUBSTEPS = 2
NLAT = 1024


def draw_cutoffs(key, part):
    values = jax.random.randint(key, (NLAT // 2,), KW // 8, KW + 1, dtype=jnp.int32)
    values = values.at[0].set(KW)
    return values.at[1].set(KW // 8)


def block_scale(stream_key, dims, cuts, least, top_value):
    def one(position, parts):
        heights = jax.random.uniform(jax.random.fold_in(jax.random.fold_in(stream_key, 6), position), (parts,), jnp.float32, least / len(cuts), top_value / len(cuts))
        return jnp.repeat(jnp.exp(heights), dims[position] // parts).reshape((-1,) + (1,) * (len(dims) - position - 1))

    level = one(*cuts[0])
    for cut in cuts[1:]:
        level = level * one(*cut)
    return level


def scatter_about(rng, dims, scale, bound, shards=(), held_as=jnp.bfloat16):
    entries = scale * jax.random.normal(rng, dims, jnp.float32)
    if shards:
        entries = entries * block_scale(rng, dims, shards, -0.22, 0.18)
    return jnp.clip(entries, -bound, bound).astype(held_as)


def setup_inputs(seed: int = 0) -> dict:
    seeds = jax.random.split(jax.random.key(seed), 6)
    return {
        "thickness": jnp.clip(0.5 + 1.0 * jax.random.uniform(seeds[0], (LEV, NLON, NLAT), jnp.float32) ** block_scale(seeds[0], (LEV, NLON, NLAT), ((1, 16), (2, 8)), -0.2, 0.2), 0.5, 1.5),
        "tracer_mass": scatter_about(seeds[1], (LEV, NLON, NLAT), 1.0, 6.0, ((1, 16), (2, 8)), jnp.float32),
        "zonal_courant": jnp.clip(jax.random.uniform(seeds[2], (LEV, NLON, NLAT), jnp.float32, -0.45, 0.45) * block_scale(seeds[2], (LEV, NLON, NLAT), ((1, 16), (2, 8)), -0.4, 0.0), -0.45, 0.45),
        "merid_courant": jnp.clip(jax.random.uniform(seeds[3], (LEV, NLON, NLAT), jnp.float32, -0.45, 0.45) * block_scale(seeds[3], (LEV, NLON, NLAT), ((1, 16), (2, 8)), -0.4, 0.0), -0.45, 0.45),
        "cutoffs": draw_cutoffs(jax.random.fold_in(seeds[5], 71), 0),
    }


def upwind(centre, east_field, west_field, north_field, south_field, zonal, east_zonal, west_zonal, merid, north_merid, south_merid):
    face_east = 0.5 * (zonal + east_zonal)
    face_west = 0.5 * (west_zonal + zonal)
    face_north = 0.5 * (merid + north_merid)
    face_south = 0.5 * (south_merid + merid)
    flux_east = jnp.maximum(face_east, 0.0) * centre + jnp.minimum(face_east, 0.0) * east_field
    flux_west = jnp.maximum(face_west, 0.0) * west_field + jnp.minimum(face_west, 0.0) * centre
    flux_north = jnp.maximum(face_north, 0.0) * centre + jnp.minimum(face_north, 0.0) * north_field
    flux_south = jnp.maximum(face_south, 0.0) * south_field + jnp.minimum(face_south, 0.0) * centre
    return centre - (flux_east - flux_west) - (flux_north - flux_south)


def advect(field, zonal, merid):
    half_turn = field.shape[2] // 2
    south_field = jnp.roll(field[:, :1], -half_turn, axis=2)
    north_field = jnp.roll(field[:, -1:], -half_turn, axis=2)
    south_merid = -jnp.roll(merid[:, :1], -half_turn, axis=2)
    north_merid = -jnp.roll(merid[:, -1:], -half_turn, axis=2)
    field_ext = jnp.concatenate([south_field, field, north_field], axis=1)
    merid_ext = jnp.concatenate([south_merid, merid, north_merid], axis=1)
    east_field = jnp.roll(field, -1, axis=2)
    west_field = jnp.roll(field, 1, axis=2)
    east_zonal = jnp.roll(zonal, -1, axis=2)
    west_zonal = jnp.roll(zonal, 1, axis=2)
    return upwind(field, east_field, west_field, field_ext[:, 2:], field_ext[:, :-2], zonal, east_zonal, west_zonal, merid, merid_ext[:, 2:], merid_ext[:, :-2])


def polar_filter(field, cutoffs):
    total_lat = field.shape[1]
    points = field.shape[2]
    quarter_rows = total_lat // 4
    polar_rows = jnp.concatenate([field[:, :quarter_rows], field[:, total_lat - quarter_rows:]], axis=1)
    spectrum = jnp.fft.rfft(polar_rows, axis=2)
    waves = jnp.arange(spectrum.shape[2], dtype=jnp.int32)
    keep_wave = waves[None, :] < cutoffs[:, None]
    spectrum = jnp.where(keep_wave[None], spectrum, 0.0)
    restored = jnp.fft.irfft(spectrum, n=points, axis=2)
    return jnp.concatenate([restored[:, :quarter_rows], field[:, quarter_rows:total_lat - quarter_rows], restored[:, quarter_rows:]], axis=1)


def reference(thickness, tracer_mass, zonal_courant, merid_courant, cutoffs):
    thickness = jnp.transpose(thickness, (0, 2, 1))
    tracer_mass = jnp.transpose(tracer_mass, (0, 2, 1))
    zonal_courant = jnp.transpose(zonal_courant, (0, 2, 1))
    merid_courant = jnp.transpose(merid_courant, (0, 2, 1))
    for substep in range(SUBSTEPS):
        thickness = polar_filter(advect(thickness, zonal_courant, merid_courant), cutoffs)
        tracer_mass = polar_filter(advect(tracer_mass, zonal_courant, merid_courant), cutoffs)
    return jnp.transpose(thickness, (0, 2, 1)), jnp.transpose(tracer_mass, (0, 2, 1))
```

```python
import functools

import jax
import jax.numpy as jnp
import ml_dtypes
import numpy as np
from jax import lax
from jax.experimental import pallas as pl
from jax.experimental.pallas import tpu as pltpu
from jax.sharding import PartitionSpec as P

KW = 256
SUBSTEPS = 2
PLANE = 8
ROUNDS = 4
MESH = pl.DeviceIdType.MESH


def split_table(table):
    high = table.astype(ml_dtypes.bfloat16)
    low = (table - high.astype(np.float64)).astype(ml_dtypes.bfloat16)
    return high, low


def dft_tables(columns, padded, inverse_rows):
    points = columns * PLANE * 2
    longitude = np.arange(PLANE * columns).reshape(PLANE, columns, 1)
    angle = (longitude * np.arange(KW) % points) * (2.0 * np.pi / points)
    table = np.concatenate([np.cos(angle), np.sin(angle)], axis=2)
    forward = np.zeros((PLANE, padded, 2 * KW))
    forward[:, :columns] = table
    inverse = np.zeros((PLANE, inverse_rows, 2 * KW))
    inverse[:, :columns] = table
    forward = forward.reshape(PLANE * padded, 2 * KW).T.copy()
    return split_table(forward) + split_table(inverse.reshape(PLANE * inverse_rows, 2 * KW))


def halves(value):
    high = value.astype(jnp.bfloat16)
    return high, (value - high.astype(jnp.float32)).astype(jnp.bfloat16)


def product(left_high, left_low, right):
    right_high, right_low = halves(right)
    dot = functools.partial(jnp.dot, preferred_element_type=jnp.float32)
    return dot(left_high, right_high) + dot(left_high, right_low) + dot(left_low, right_high)


def kernel(
    columns, padded, inverse_rows,
    thick_in, tracer_in, zonal_in, merid_in, keep, fwd_hi, fwd_lo, inv_hi, inv_lo,
    thick_out, tracer_out,
    field, zonal, merid, adv, circle, back, passed, spec, spec_in, edge, edge_in, rim, rim_in,
    in_sem, out_sem, halo_send, edge_recv, rim_recv, mig_send, mig_recv, fwd_send, fwd_recv,
    swap_send, swap_recv, ret_send, ret_recv, home_send, home_recv,
):
    band = lax.axis_index("lat")
    lon = lax.axis_index("lon")
    mine = lon % PLANE
    plane = lon - mine
    across = (lon + PLANE) % (2 * PLANE)
    east = (lon + 1) % (2 * PLANE)
    west = (lon + 2 * PLANE - 1) % (2 * PLANE)
    last_band = band // 7
    first_band = 1 - (band + 7) // 8
    helper_x = (band // 4) * 4 + 3 - band % 4
    helper_z = (band + 4) % 8
    polar = (band < 2) | (band >= 6)

    loads = [
        pltpu.make_async_copy(thick_in, field.at[:, :, 0, pl.ds(0, columns)], in_sem.at[0]),
        pltpu.make_async_copy(tracer_in, field.at[:, :, 1, pl.ds(0, columns)], in_sem.at[1]),
        pltpu.make_async_copy(zonal_in, zonal.at[:, :, pl.ds(0, columns)], in_sem.at[2]),
        pltpu.make_async_copy(merid_in, merid.at[:, :, pl.ds(0, columns)], in_sem.at[3]),
    ]
    for load in loads:
        load.start()

    barrier = pltpu.get_barrier_semaphore()
    partners = [(band, plane + (mine + step) % PLANE) for step in range(1, PLANE)]
    partners += [(band, across), (band, east), (band, west)]
    partners += [((band + 1) % 8, lon), ((band + 7) % 8, lon), (helper_x, lon), (helper_z, across)]
    for partner in partners:
        pl.semaphore_signal(barrier, inc=1, device_id=partner, device_id_type=MESH)

    row = lax.broadcasted_iota(jnp.int32, (padded, 128), 0)
    lane = lax.broadcasted_iota(jnp.int32, (padded, 128), 1)
    tail = jnp.zeros((padded - columns, 128), jnp.float32)

    def clear(index, carry):
        group, level = index // PLANE, index % PLANE
        field[group, level, 0, pl.ds(columns, padded - columns)] = tail
        field[group, level, 1, pl.ds(columns, padded - columns)] = tail
        zonal[group, level, pl.ds(columns, padded - columns)] = tail
        merid[group, level, pl.ds(columns, padded - columns)] = tail
        return carry

    lax.fori_loop(0, ROUNDS * PLANE, clear, 0)
    for load in loads:
        load.wait()
    pl.semaphore_wait(barrier, len(partners))

    def remote(src, dst, send, recv, device):
        return pltpu.make_async_remote_copy(
            src_ref=src, dst_ref=dst, send_sem=send, recv_sem=recv, device_id=device, device_id_type=MESH
        )

    def halo_copies(step, group):
        return [
            remote(rim.at[step, group, 1], rim_in.at[step, group, 0], halo_send.at[step, group, 0],
                   rim_recv.at[step, group, 0], (band, east)),
            remote(rim.at[step, group, 0], rim_in.at[step, group, 1], halo_send.at[step, group, 1],
                   rim_recv.at[step, group, 1], (band, west)),
            remote(edge.at[step, group], edge_in.at[step, group, last_band], halo_send.at[step, group, 2],
                   edge_recv.at[step, group, last_band],
                   (band + 1 - last_band, (lon + PLANE * last_band) % (2 * PLANE))),
            remote(edge.at[step, group], edge_in.at[step, group, 1 - first_band], halo_send.at[step, group, 3],
                   edge_recv.at[step, group, 1 - first_band],
                   (band - 1 + first_band, (lon + PLANE * first_band) % (2 * PLANE))),
        ]

    def halo_wait(step, group):
        for side in range(2):
            remote(rim.at[step, group, 0], rim_in.at[step, group, side], halo_send.at[step, group, 0],
                   rim_recv.at[step, group, side], (band, east)).wait_recv()
            remote(edge.at[step, group], edge_in.at[step, group, side], halo_send.at[step, group, 0],
                   edge_recv.at[step, group, side], (band, across)).wait_recv()

    def pack(step, group):
        def one(level, packed):
            values = [field[group, level, 0], field[group, level, 1]]
            if step == 0:
                values.append(merid[group, level])
            for array, value in enumerate(values):
                place = array * PLANE + level
                packed = jnp.where(lane == place, pltpu.roll(value, place, 1), packed)
                packed = jnp.where(lane == 64 + place, pltpu.roll(value, 65 + place, 1), packed)
            rows = [field.at[group, level, 0], field.at[group, level, 1]]
            if step == 0:
                rows.append(zonal.at[group, level])
            for array, ref in enumerate(rows):
                place = array * PLANE + level
                rim[step, group, 0, pl.ds(place, 1)] = ref[pl.ds(0, 1)]
                rim[step, group, 1, pl.ds(place, 1)] = ref[pl.ds(columns - 1, 1)]
            return packed

        edge[step, group] = lax.fori_loop(0, PLANE, one, jnp.zeros((padded, 128), jnp.float32))
        for copy in halo_copies(step, group):
            copy.start()

    sign_south = 1.0 - 2.0 * first_band.astype(jnp.float32)
    sign_north = 1.0 - 2.0 * last_band.astype(jnp.float32)
    south_place = 64 * (1 - first_band)
    north_place = 64 * last_band

    def advect(step, group, level):
        def eastward(value, halo):
            return jnp.where(row == columns - 1, halo, pltpu.roll(value, padded - 1, 0))

        def rims(at, place):
            return rim_in[at, group, 0, pl.ds(place, 1)], rim_in[at, group, 1, pl.ds(place, 1)]

        def northward(at, place, value, sign):
            column = pltpu.roll(edge_in[at, group, 1], 127 - north_place - place, 1)
            return jnp.where(lane == 127, column if sign is None else sign * column, pltpu.roll(value, 127, 1))

        def southward(at, place, value, sign):
            column = pltpu.roll(edge_in[at, group, 0], 128 - south_place - place, 1)
            return jnp.where(lane == 0, column if sign is None else sign * column, pltpu.roll(value, 1, 1))

        a = zonal[group, level]
        m = merid[group, level]
        west_a, east_a = rims(0, 2 * PLANE + level)
        face_east = 0.5 * (a + eastward(a, east_a))
        face_west = 0.5 * (west_a + a[0:1])
        face_north = 0.5 * (m + northward(0, 2 * PLANE + level, m, sign_north))
        face_south = 0.5 * (southward(0, 2 * PLANE + level, m, sign_south) + m)
        results = []
        for array in range(2):
            f = field[group, level, array]
            place = array * PLANE + level
            west_f, east_f = rims(step, place)
            flux_east = jnp.maximum(face_east, 0.0) * f + jnp.minimum(face_east, 0.0) * eastward(f, east_f)
            first_west = jnp.maximum(face_west, 0.0) * west_f + jnp.minimum(face_west, 0.0) * f[0:1]
            flux_west = jnp.where(row == 0, first_west, pltpu.roll(flux_east, 1, 0))
            flux_north = jnp.maximum(face_north, 0.0) * f + jnp.minimum(face_north, 0.0) * northward(step, place, f, None)
            flux_south = jnp.maximum(face_south, 0.0) * southward(step, place, f, None) + jnp.minimum(face_south, 0.0) * f
            result = f - (flux_east - flux_west) - (flux_north - flux_south)
            results.append(jnp.where(row < columns, result, 0.0))
        return results

    def mig_copy(job, level, device):
        return remote(adv.at[2 + job, level], adv.at[job, level], mig_send.at[job, level], mig_recv.at[job, level], device)

    def fwd_copy(job, level):
        return remote(adv.at[job, level], circle.at[job, mine], fwd_send.at[job, level], fwd_recv.at[job, mine],
                      (band, plane + level))

    def own_copy(job):
        return pltpu.make_async_copy(adv.at[job, mine], circle.at[job, mine], fwd_send.at[job, mine])

    def swap_copy(step, job):
        return remote(spec.at[job], spec_in.at[step, job], swap_send.at[job], swap_recv.at[job], (band, across))

    def ret_copy(job, other, target):
        return remote(back.at[job, other], target.at[job, mine], ret_send.at[job, other], ret_recv.at[job, mine],
                      (band, plane + other))

    def home_copy(job, level):
        device = (helper_x, lon) if job == 0 else (helper_z, across)
        return remote(passed.at[job, level], field.at[2 + job, level], home_send.at[job, level], home_recv.at[job, level],
                      device)

    def loop(count, body):
        def run(index, carry):
            body(index)
            return carry

        lax.fori_loop(0, count, run, 0)

    wave_row = lax.broadcasted_iota(jnp.int32, (2 * KW, 256), 0)
    parity = 1.0 - 2.0 * (wave_row % 2).astype(jnp.float32)

    for step in range(SUBSTEPS):
        for group in range(ROUNDS):
            pack(step, group)
        for group in range(ROUNDS):
            halo_wait(step, group)

        def advect_one(index, step=step):
            group = (index + 2) % ROUNDS
            level = (mine + index // ROUNDS) % PLANE
            first, second = advect(step, group, level)

            @pl.when(polar)
            def _():
                adv[group, level, 0] = first
                adv[group, level, 1] = second

                @pl.when(group == 2)
                def _():
                    mig_copy(0, level, (helper_x, lon)).start()

                @pl.when(group == 3)
                def _():
                    mig_copy(1, level, (helper_z, across)).start()

            @pl.when(jnp.logical_not(polar))
            def _():
                field[group, level, 0] = first
                field[group, level, 1] = second

                @pl.when(group < 2)
                def _():
                    mig_copy(group, level, (helper_x, lon)).wait_recv()

            @pl.when((group < 2) & (level != mine))
            def _():
                fwd_copy(group, level).start()

            @pl.when((group < 2) & (level == mine))
            def _():
                own_copy(group).start()

        loop(ROUNDS * PLANE, advect_one)

        for job in range(2):
            def arrived(index, job=job):
                source = (mine + PLANE - 1 - index) % PLANE
                remote(adv.at[job, source], circle.at[job, source], fwd_send.at[job, source], fwd_recv.at[job, source],
                       (band, plane + source)).wait_recv()

            own_copy(job).wait()
            loop(PLANE - 1, arrived)
            both = jnp.concatenate(
                [circle[job, :, 0].reshape(PLANE * padded, 128), circle[job, :, 1].reshape(PLANE * padded, 128)], axis=1
            )
            spec[job] = product(fwd_hi[...], fwd_lo[...], both)
            swap_copy(step, job).start()

        for job in range(2):
            swap_copy(step, job).wait_recv()
            weight = keep[job]
            weight = jnp.concatenate([weight, weight], axis=1)
            kept_hi, kept_lo = halves((spec[job] + parity * spec_in[step, job]) * weight)

            def give(index, job=job, kept_hi=kept_hi, kept_lo=kept_lo):
                other = (mine + 1 + index) % PLANE
                place = pl.ds(pl.multiple_of(other * inverse_rows, inverse_rows), inverse_rows)
                dot = functools.partial(jnp.dot, preferred_element_type=jnp.float32)
                value = dot(inv_hi[place], kept_hi) + dot(inv_hi[place], kept_lo) + dot(inv_lo[place], kept_hi)
                back[job, other, 0] = value[:padded, :128]
                back[job, other, 1] = value[:padded, 128:]

                @pl.when((other != mine) & polar)
                def _():
                    ret_copy(job, other, field).start()

                @pl.when((other != mine) & jnp.logical_not(polar))
                def _():
                    ret_copy(job, other, passed).start()

            loop(PLANE, give)

            @pl.when(polar)
            def _(job=job):
                field[job, mine] = back[job, mine]

            @pl.when(jnp.logical_not(polar))
            def _(job=job):
                passed[job, mine] = back[job, mine]

        for job in range(2):
            def fwd_done(index, job=job):
                fwd_copy(job, (mine + 1 + index) % PLANE).wait_send()

            loop(PLANE - 1, fwd_done)

        @pl.when(jnp.logical_not(polar))
        def _():
            for job in range(2):
                home_copy(job, mine).start()

            def forward(index):
                source = (mine + PLANE - 1 - index) % PLANE
                for job in range(2):
                    remote(back.at[job, source], passed.at[job, source], ret_send.at[job, source],
                           ret_recv.at[job, source], (band, plane + source)).wait_recv()
                    home_copy(job, source).start()

            loop(PLANE - 1, forward)

            def sent(index):
                for job in range(2):
                    home_copy(job, index).wait_send()

            loop(PLANE, sent)

        @pl.when(polar)
        def _():
            def landed(index):
                source = (mine + PLANE - 1 - index) % PLANE
                for job in range(2):
                    remote(back.at[job, source], field.at[job, source], ret_send.at[job, source],
                           ret_recv.at[job, source], (band, plane + source)).wait_recv()

            loop(PLANE - 1, landed)

            def home(index):
                for job in range(2):
                    mig_copy(job, index, (helper_x, lon)).wait_send()
                    home_copy(job, index).wait_recv()

            loop(PLANE, home)

        def ret_done(index):
            for job in range(2):
                ret_copy(job, (mine + 1 + index) % PLANE, passed).wait_send()

        loop(PLANE - 1, ret_done)
        for job in range(2):
            swap_copy(step, job).wait_send()
        for group in range(ROUNDS):
            for copy in halo_copies(step, group):
                copy.wait_send()

    stores = [
        pltpu.make_async_copy(field.at[:, :, 0, pl.ds(0, columns)], thick_out, out_sem.at[0]),
        pltpu.make_async_copy(field.at[:, :, 1, pl.ds(0, columns)], tracer_out, out_sem.at[1]),
    ]
    for store in stores:
        store.start()
    for store in stores:
        store.wait()


def kept_waves(cutoffs, source_band, lat_rows, points):
    quarter_rows = cutoffs.shape[0] // 2
    latitude = source_band * lat_rows + jnp.arange(lat_rows, dtype=jnp.int32)
    polar_index = jnp.where(latitude < quarter_rows, latitude, latitude - 2 * quarter_rows)
    slots = jnp.arange(cutoffs.shape[0], dtype=jnp.int32)
    row_cut = jnp.sum(jnp.where(polar_index[:, None] == slots[None, :], cutoffs[None, :], 0), axis=1)
    wave = jnp.arange(KW, dtype=jnp.int32)
    weight = (jnp.where(wave == 0, 1.0, 2.0) / points).astype(jnp.float32)
    kept = jnp.where(wave[:, None] < row_cut[None, :], weight[:, None], 0.0)
    return jnp.concatenate([kept, kept], axis=0)


def on_device(thickness, tracer_mass, zonal_courant, merid_courant, cutoffs):
    band = lax.axis_index("lat")
    levels, columns, lat_rows = thickness.shape
    points = columns * lax.axis_size("lon")
    padded = -(-columns // 8) * 8
    inverse_rows = -(-columns // 16) * 16
    polar = (band < 2) | (band >= 6)
    helped_x = (band // 4) * 4 + 3 - band % 4
    helped_z = (band + 4) % 8
    keep = jnp.stack(
        [
            kept_waves(cutoffs, jnp.where(polar, band, helped_x), lat_rows, points),
            kept_waves(cutoffs, jnp.where(polar, band, helped_z), lat_rows, points),
        ]
    )
    tables = [jnp.asarray(table) for table in dft_tables(columns, padded, inverse_rows)]
    shape = (ROUNDS, PLANE, columns, lat_rows)
    f32 = jnp.float32
    dma = pltpu.SemaphoreType.DMA
    piece = (2, padded, 128)
    outs = pl.pallas_call(
        functools.partial(kernel, columns, padded, inverse_rows),
        out_shape=[jax.ShapeDtypeStruct(shape, f32)] * 2,
        in_specs=[pl.BlockSpec(memory_space=pl.ANY)] * 4 + [pl.BlockSpec(memory_space=pltpu.VMEM)] * 5,
        out_specs=[pl.BlockSpec(memory_space=pl.ANY)] * 2,
        scratch_shapes=[
            pltpu.VMEM((ROUNDS, PLANE) + piece, f32),
            pltpu.VMEM((ROUNDS, PLANE, padded, 128), f32),
            pltpu.VMEM((ROUNDS, PLANE, padded, 128), f32),
            pltpu.VMEM((ROUNDS, PLANE) + piece, f32),
            pltpu.VMEM((2, PLANE) + piece, f32),
            pltpu.VMEM((2, PLANE) + piece, f32),
            pltpu.VMEM((2, PLANE) + piece, f32),
            pltpu.VMEM((2, 2 * KW, 256), f32),
            pltpu.VMEM((SUBSTEPS, 2, 2 * KW, 256), f32),
            pltpu.VMEM((SUBSTEPS, ROUNDS, padded, 128), f32),
            pltpu.VMEM((SUBSTEPS, ROUNDS, 2, padded, 128), f32),
            pltpu.VMEM((SUBSTEPS, ROUNDS, 2, 3 * PLANE, 128), f32),
            pltpu.VMEM((SUBSTEPS, ROUNDS, 2, 3 * PLANE, 128), f32),
            dma((4,)),
            dma((2,)),
            dma((SUBSTEPS, ROUNDS, 4)),
            dma((SUBSTEPS, ROUNDS, 2)),
            dma((SUBSTEPS, ROUNDS, 2)),
            dma((2, PLANE)),
            dma((2, PLANE)),
            dma((2, PLANE)),
            dma((2, PLANE)),
            dma((2,)),
            dma((2,)),
            dma((2, PLANE)),
            dma((2, PLANE)),
            dma((2, PLANE)),
            dma((2, PLANE)),
        ],
        compiler_params=pltpu.CompilerParams(
            collective_id=0, has_side_effects=True, vmem_limit_bytes=60 * 1024 * 1024
        ),
    )(
        thickness.reshape(shape),
        tracer_mass.reshape(shape),
        zonal_courant.reshape(shape),
        merid_courant.reshape(shape),
        keep,
        *tables,
    )
    return outs[0].reshape(thickness.shape), outs[1].reshape(thickness.shape)


def solution(mesh):
    placed = P(None, "lon", "lat")
    return jax.shard_map(
        on_device,
        mesh=mesh,
        in_specs=(placed, placed, placed, placed, P()),
        out_specs=(placed, placed),
        check_vma=False,
    )
```

```python
import functools

import jax
import jax.numpy as jnp
import ml_dtypes
import numpy as np
from jax import lax
from jax.experimental import pallas as pl
from jax.experimental.pallas import tpu as pltpu
from jax.sharding import PartitionSpec as P

KW = 256
SUBSTEPS = 2
PLANE = 8
ROUNDS = 4
CHIPS = PLANE // 2
MESH = pl.DeviceIdType.MESH


def split_table(table):
    high = table.astype(ml_dtypes.bfloat16)
    low = (table - high.astype(np.float64)).astype(ml_dtypes.bfloat16)
    return high, low


def dft_tables(columns, padded, inverse_rows):
    points = columns * PLANE * 2
    longitude = np.arange(PLANE * columns).reshape(PLANE, columns, 1)
    angle = (longitude * np.arange(KW) % points) * (2.0 * np.pi / points)
    table = np.concatenate([np.cos(angle), np.sin(angle)], axis=2)
    forward = np.zeros((PLANE, padded, 2 * KW))
    forward[:, :columns] = table
    inverse = np.zeros((PLANE, inverse_rows, 2 * KW))
    inverse[:, :columns] = table
    forward = forward.reshape(PLANE * padded, 2 * KW).T.copy()
    return split_table(forward) + split_table(inverse.reshape(PLANE * inverse_rows, 2 * KW))


def halves(value):
    high = value.astype(jnp.bfloat16)
    return high, (value - high.astype(jnp.float32)).astype(jnp.bfloat16)


def dot(left, right):
    return jnp.dot(left, right, preferred_element_type=jnp.float32)


def product(left_high, left_low, right):
    right_high, right_low = halves(right)
    return dot(left_high, right_high) + dot(left_high, right_low) + dot(left_low, right_high)


def kernel(
    columns, padded, inverse_rows,
    thick_in, tracer_in, zonal_in, merid_in, keep, fwd_hi, fwd_lo, inv_hi, inv_lo,
    thick_out, tracer_out,
    field, zonal, merid, adv, circle, back, passed, spec, spec_in, edge, edge_in, rim, rim_in,
    in_sem, out_sem, halo_send, edge_recv, rim_recv, mig_send, mig_recv, fwd_send, fwd_recv,
    swap_send, swap_recv, ret_send, ret_recv, home_send, home_recv,
):
    band = lax.axis_index("lat")
    lon = lax.axis_index("lon")
    mine = lon % PLANE
    plane = lon - mine
    chip = mine // 2
    across = (lon + PLANE) % (2 * PLANE)
    east = (lon + 1) % (2 * PLANE)
    west = (lon + 2 * PLANE - 1) % (2 * PLANE)
    last_band = band // 7
    first_band = 1 - (band + 7) // 8
    helper_x = (band // 4) * 4 + 3 - band % 4
    helper_z = (band + 4) % 8
    polar = (band < 2) | (band >= 6)
    helping = jnp.logical_not(polar)

    def loop(count, body):
        def run(index, carry):
            body(index)
            return carry

        lax.fori_loop(0, count, run, 0)

    def inner(ref, *place):
        return ref.at[place + (pl.ds(0, columns),)]

    def load_copies(group, level):
        height = group * PLANE + level
        half, slab = level // CHIPS, 2 * (level % CHIPS)
        return [
            pltpu.make_async_copy(thick_in.at[:, height], inner(field, half, group, slab), in_sem.at[group, level, 0]),
            pltpu.make_async_copy(tracer_in.at[:, height], inner(field, half, group, slab + 1), in_sem.at[group, level, 1]),
            pltpu.make_async_copy(zonal_in.at[:, height], inner(zonal, group, level), in_sem.at[group, level, 2]),
            pltpu.make_async_copy(merid_in.at[:, height], inner(merid, group, level), in_sem.at[group, level, 3]),
        ]

    def store_copies(group, level):
        height = group * PLANE + level
        half, slab = level // CHIPS, 2 * (level % CHIPS)
        return [
            pltpu.make_async_copy(inner(field, half, group, slab), thick_out.at[:, height], out_sem.at[group, level, 0]),
            pltpu.make_async_copy(inner(field, half, group, slab + 1), tracer_out.at[:, height], out_sem.at[group, level, 1]),
        ]

    def load(index):
        for copy in load_copies(index // PLANE, index % PLANE):
            copy.start()

    loop(ROUNDS * PLANE, load)

    barrier = pltpu.get_barrier_semaphore()
    partners = [(band, plane + (mine + step) % PLANE) for step in range(1, PLANE)]
    partners += [(band, across), (band, east), (band, west)]
    partners += [((band + 1) % 8, lon), ((band + 7) % 8, lon), (helper_x, lon), (helper_z, across)]
    for partner in partners:
        pl.semaphore_signal(barrier, inc=1, device_id=partner, device_id_type=MESH)

    row = lax.broadcasted_iota(jnp.int32, (padded, 128), 0)
    lane = lax.broadcasted_iota(jnp.int32, (padded, 128), 1)
    rest = pl.ds(columns, padded - columns)
    blank = jnp.zeros((padded - columns, 128), jnp.float32)

    def clear(index):
        group, level = index // PLANE, index % PLANE
        field[0, group, level, rest] = blank
        field[1, group, level, rest] = blank
        zonal[group, level, rest] = blank
        merid[group, level, rest] = blank

    loop(ROUNDS * PLANE, clear)
    pl.semaphore_wait(barrier, len(partners))

    def remote(src, dst, send, recv, device):
        return pltpu.make_async_remote_copy(
            src_ref=src, dst_ref=dst, send_sem=send, recv_sem=recv, device_id=device, device_id_type=MESH
        )

    def halo_copies(step, group):
        return [
            remote(rim.at[step, group, 1], rim_in.at[step, group, 0], halo_send.at[step, group, 0],
                   rim_recv.at[step, group, 0], (band, east)),
            remote(rim.at[step, group, 0], rim_in.at[step, group, 1], halo_send.at[step, group, 1],
                   rim_recv.at[step, group, 1], (band, west)),
            remote(edge.at[step, group], edge_in.at[step, group, last_band], halo_send.at[step, group, 2],
                   edge_recv.at[step, group, last_band],
                   (band + 1 - last_band, (lon + PLANE * last_band) % (2 * PLANE))),
            remote(edge.at[step, group], edge_in.at[step, group, 1 - first_band], halo_send.at[step, group, 3],
                   edge_recv.at[step, group, 1 - first_band],
                   (band - 1 + first_band, (lon + PLANE * first_band) % (2 * PLANE))),
        ]

    def halo_wait(step, group):
        for side in range(2):
            remote(rim.at[step, group, 0], rim_in.at[step, group, side], halo_send.at[step, group, 0],
                   rim_recv.at[step, group, side], (band, east)).wait_recv()
            remote(edge.at[step, group], edge_in.at[step, group, side], halo_send.at[step, group, 0],
                   edge_recv.at[step, group, side], (band, across)).wait_recv()

    def pack(step, group):
        def one(level, packed):
            half, slab = level // CHIPS, 2 * (level % CHIPS)
            values = [field[half, group, slab], field[half, group, slab + 1], merid[group, level]]
            for array, value in enumerate(values):
                place = array * PLANE + level
                packed = jnp.where(lane == place, pltpu.roll(value, place, 1), packed)
                packed = jnp.where(lane == 64 + place, pltpu.roll(value, 65 + place, 1), packed)
            rows = [field.at[half, group, slab], field.at[half, group, slab + 1], zonal.at[group, level]]
            for array, ref in enumerate(rows):
                place = array * PLANE + level
                rim[step, group, 0, pl.ds(place, 1)] = ref[pl.ds(0, 1)]
                rim[step, group, 1, pl.ds(place, 1)] = ref[pl.ds(columns - 1, 1)]
            return packed

        edge[step, group] = lax.fori_loop(0, PLANE, one, jnp.zeros((padded, 128), jnp.float32))
        for copy in halo_copies(step, group):
            copy.start()

    sign_south = 1.0 - 2.0 * first_band.astype(jnp.float32)
    sign_north = 1.0 - 2.0 * last_band.astype(jnp.float32)
    south_place = 64 * (1 - first_band)
    north_place = 64 * last_band

    def advect(step, group, level):
        half, slab = level // CHIPS, 2 * (level % CHIPS)

        def eastward(value, halo):
            return jnp.where(row == columns - 1, halo, pltpu.roll(value, padded - 1, 0))

        def rims(place):
            return rim_in[step, group, 0, pl.ds(place, 1)], rim_in[step, group, 1, pl.ds(place, 1)]

        def northward(place, value, sign):
            column = pltpu.roll(edge_in[step, group, 1], 127 - north_place - place, 1)
            return jnp.where(lane == 127, column if sign is None else sign * column, pltpu.roll(value, 127, 1))

        def southward(place, value, sign):
            column = pltpu.roll(edge_in[step, group, 0], 128 - south_place - place, 1)
            return jnp.where(lane == 0, column if sign is None else sign * column, pltpu.roll(value, 1, 1))

        a = zonal[group, level]
        m = merid[group, level]
        west_a, east_a = rims(2 * PLANE + level)
        face_east = 0.5 * (a + eastward(a, east_a))
        face_west = 0.5 * (west_a + a[0:1])
        face_north = 0.5 * (m + northward(2 * PLANE + level, m, sign_north))
        face_south = 0.5 * (southward(2 * PLANE + level, m, sign_south) + m)
        results = []
        for array in range(2):
            f = field[half, group, slab + array]
            place = array * PLANE + level
            west_f, east_f = rims(place)
            flux_east = jnp.maximum(face_east, 0.0) * f + jnp.minimum(face_east, 0.0) * eastward(f, east_f)
            first_west = jnp.maximum(face_west, 0.0) * west_f + jnp.minimum(face_west, 0.0) * f[0:1]
            flux_west = jnp.where(row == 0, first_west, pltpu.roll(flux_east, 1, 0))
            flux_north = jnp.maximum(face_north, 0.0) * f + jnp.minimum(face_north, 0.0) * northward(place, f, None)
            flux_south = jnp.maximum(face_south, 0.0) * southward(place, f, None) + jnp.minimum(face_south, 0.0) * f
            result = f - (flux_east - flux_west) - (flux_north - flux_south)
            results.append(jnp.where(row < columns, result, 0.0))
        return results


    def mig_copy(unit, place, device):
        pair = pl.ds(2 * place, 2)
        return remote(adv.at[1, unit, pair], adv.at[0, unit, pair], mig_send.at[unit, place], mig_recv.at[unit, place],
                      device)

    def fwd_copy(unit, slab):
        return remote(adv.at[0, unit, slab], circle.at[unit, mine], fwd_send.at[unit, slab], fwd_recv.at[unit, mine],
                      (band, plane + slab))

    def own_copy(unit):
        return pltpu.make_async_copy(adv.at[0, unit, mine], circle.at[unit, mine], fwd_send.at[unit, mine])

    def swap_copy(step, unit):
        return remote(spec.at[unit], spec_in.at[step, unit], swap_send.at[unit], swap_recv.at[unit], (band, across))

    def ret_copy(unit, other, target):
        return remote(back.at[unit, other], target.at[unit, mine], ret_send.at[unit, other], ret_recv.at[unit, mine],
                      (band, plane + other))

    def home_copy(unit, slab, device):
        return remote(passed.at[unit, slab], field.at[1, unit, slab], home_send.at[unit, slab], home_recv.at[unit, slab],
                      device)

    def send_forward(unit, slab):
        @pl.when(slab != mine)
        def _():
            fwd_copy(unit, slab).start()

        @pl.when(slab == mine)
        def _():
            own_copy(unit).start()

    def given(unit):
        def one(index):
            ret_copy(unit, (mine + 1 + index) % PLANE, passed).wait_send()

        loop(PLANE - 1, one)

    def handed(unit):
        def one(slab):
            home_copy(unit, slab, (helper_x, lon)).wait_send()

        given(unit)
        loop(PLANE, one)

    def prepare(item):
        step, unit = item // ROUNDS, item % ROUNDS

        @pl.when(step == 0)
        def _():
            def loaded(level):
                for copy in load_copies(unit, level):
                    copy.wait()

            loop(PLANE, loaded)

        @pl.when((step > 0) & polar)
        def _():
            def landed(index):
                source = (mine + PLANE - 1 - index) % PLANE
                remote(back.at[unit, source], field.at[0, unit, source], ret_send.at[unit, source],
                       ret_recv.at[unit, source], (band, plane + source)).wait_recv()

            def sent(place):
                mig_copy(unit, place, (helper_x, lon)).wait_send()

            def home(slab):
                home_copy(unit, slab, (helper_x, lon)).wait_recv()

            given(unit)
            loop(PLANE - 1, landed)
            loop(CHIPS, sent)
            loop(PLANE, home)

        @pl.when(step < SUBSTEPS)
        def _():
            pack(step, unit)

        @pl.when(step == SUBSTEPS)
        def _():
            def store(level):
                for copy in store_copies(unit, level):
                    copy.start()

            loop(PLANE, store)

    def advance(item):
        step, unit = item // ROUNDS, item % ROUNDS
        halo_wait(step, unit)

        def one(index):
            half = 1 - index % 2
            place = (chip + 1 + index // 2) % CHIPS
            slab = 2 * place
            first, second = advect(step, unit, half * CHIPS + place)

            @pl.when(helping)
            def _():
                field[half, unit, slab] = first
                field[half, unit, slab + 1] = second

            @pl.when(polar)
            def _():
                adv[half, unit, slab] = first
                adv[half, unit, slab + 1] = second

                @pl.when((half == 1) & (place < CHIPS // 2))
                def _():
                    mig_copy(unit, place, (helper_x, lon)).start()

                @pl.when((half == 1) & (place >= CHIPS // 2))
                def _():
                    mig_copy(unit, place, (helper_z, across)).start()

                @pl.when(half == 0)
                def _():
                    send_forward(unit, slab)
                    send_forward(unit, slab + 1)

        loop(PLANE, one)

    def relay(item):
        unit = item % ROUNDS

        @pl.when(item >= ROUNDS)
        def _():
            handed(unit)

        def one(index):
            place = (chip + 1 + index) % CHIPS
            mig_copy(unit, place, (helper_x, lon)).wait_recv()
            send_forward(unit, 2 * place)
            send_forward(unit, 2 * place + 1)

        loop(CHIPS, one)

    def transform(item):
        step, unit = item // ROUNDS, item % ROUNDS
        own_copy(unit).wait()

        def arrived(index):
            source = (mine + PLANE - 1 - index) % PLANE
            remote(adv.at[0, unit, source], circle.at[unit, source], fwd_send.at[unit, source],
                   fwd_recv.at[unit, source], (band, plane + source)).wait_recv()

        loop(PLANE - 1, arrived)
        spec[unit] = product(fwd_hi[...], fwd_lo[...], circle[unit].reshape(PLANE * padded, 128))
        swap_copy(step, unit).start()

    wave_row = lax.broadcasted_iota(jnp.int32, (2 * KW, 128), 0)
    parity = 1.0 - 2.0 * (wave_row % 2).astype(jnp.float32)

    def restore(item):
        step, unit = item // ROUNDS, item % ROUNDS

        def sent(index):
            fwd_copy(unit, (mine + 1 + index) % PLANE).wait_send()

        loop(PLANE - 1, sent)
        swap_copy(step, unit).wait()
        kept_hi, kept_lo = halves((spec[unit] + parity * spec_in[step, unit]) * keep[mine // CHIPS])

        def give(index):
            other = (mine + 1 + index) % PLANE
            place = pl.ds(pl.multiple_of(other * inverse_rows, inverse_rows), inverse_rows)
            value = dot(inv_hi[place], kept_hi) + dot(inv_hi[place], kept_lo) + dot(inv_lo[place], kept_hi)
            value = value[:padded]

            @pl.when(other != mine)
            def _():
                back[unit, other] = value

            @pl.when((other != mine) & polar)
            def _():
                ret_copy(unit, other, field.at[0]).start()

            @pl.when((other != mine) & helping)
            def _():
                ret_copy(unit, other, passed).start()

            @pl.when((other == mine) & polar)
            def _():
                field[0, unit, mine] = value

            @pl.when((other == mine) & helping)
            def _():
                passed[unit, mine] = value

        loop(PLANE, give)

    def send_home(item):
        unit = item % ROUNDS

        def one(index):
            slab = (mine + PLANE - index) % PLANE

            @pl.when(slab != mine)
            def _():
                remote(back.at[unit, slab], passed.at[unit, slab], ret_send.at[unit, slab],
                       ret_recv.at[unit, slab], (band, plane + slab)).wait_recv()

            @pl.when(slab < CHIPS)
            def _():
                home_copy(unit, slab, (helper_x, lon)).start()

            @pl.when(slab >= CHIPS)
            def _():
                home_copy(unit, slab, (helper_z, across)).start()

        loop(PLANE, one)

    items = SUBSTEPS * ROUNDS

    def tick(time):
        @pl.when((time < items) & polar)
        def _():
            advance(time)

        @pl.when((time >= 3) & helping)
        def _():
            send_home(time - 3)

        @pl.when((time >= 2) & (time < items + 2))
        def _():
            restore(time - 2)

        @pl.when((time >= 1) & (time < items + 1))
        def _():
            transform(time - 1)

        @pl.when((time < items) & helping)
        def _():
            relay(time)
            advance(time)

        @pl.when(polar)
        def _():
            prepare(time + 1)

        @pl.when((time < items) & helping)
        def _():
            prepare(time + ROUNDS)

    @pl.when(polar)
    def _():
        prepare(0)

    @pl.when(helping)
    def _():
        loop(ROUNDS, prepare)

    loop(items + 3, tick)

    @pl.when(helping)
    def _():
        loop(ROUNDS, handed)

    def halo_done(index):
        for copy in halo_copies(index // ROUNDS, index % ROUNDS):
            copy.wait_send()

    loop(items, halo_done)

    def stored(index):
        for copy in store_copies(index // PLANE, index % PLANE):
            copy.wait()

    loop(ROUNDS * PLANE, stored)


def kept_waves(cutoffs, source_band, lat_rows, points):
    quarter_rows = cutoffs.shape[0] // 2
    latitude = source_band * lat_rows + jnp.arange(lat_rows, dtype=jnp.int32)
    polar_index = jnp.where(latitude < quarter_rows, latitude, latitude - 2 * quarter_rows)
    slots = jnp.arange(cutoffs.shape[0], dtype=jnp.int32)
    row_cut = jnp.sum(jnp.where(polar_index[:, None] == slots[None, :], cutoffs[None, :], 0), axis=1)
    wave = jnp.arange(KW, dtype=jnp.int32)
    weight = (jnp.where(wave == 0, 1.0, 2.0) / points).astype(jnp.float32)
    kept = jnp.where(wave[:, None] < row_cut[None, :], weight[:, None], 0.0)
    return jnp.concatenate([kept, kept], axis=0)


def on_device(thickness, tracer_mass, zonal_courant, merid_courant, cutoffs):
    band = lax.axis_index("lat")
    levels, columns, lat_rows = thickness.shape
    points = columns * lax.axis_size("lon")
    padded = -(-columns // 8) * 8
    inverse_rows = -(-columns // 16) * 16
    polar = (band < 2) | (band >= 6)
    helped_x = (band // 4) * 4 + 3 - band % 4
    helped_z = (band + 4) % 8
    keep = jnp.stack(
        [
            kept_waves(cutoffs, jnp.where(polar, band, helped_x), lat_rows, points),
            kept_waves(cutoffs, jnp.where(polar, band, helped_z), lat_rows, points),
        ]
    )
    tables = [jnp.asarray(table) for table in dft_tables(columns, padded, inverse_rows)]
    shape = (columns, levels, lat_rows)
    f32 = jnp.float32
    dma = pltpu.SemaphoreType.DMA
    piece = (PLANE, padded, 128)
    outs = pl.pallas_call(
        functools.partial(kernel, columns, padded, inverse_rows),
        out_shape=[jax.ShapeDtypeStruct(shape, f32)] * 2,
        in_specs=[pl.BlockSpec(memory_space=pl.ANY)] * 4 + [pl.BlockSpec(memory_space=pltpu.VMEM)] * 5,
        out_specs=[pl.BlockSpec(memory_space=pl.ANY)] * 2,
        scratch_shapes=[
            pltpu.VMEM((2, ROUNDS) + piece, f32),
            pltpu.VMEM((ROUNDS,) + piece, f32),
            pltpu.VMEM((ROUNDS,) + piece, f32),
            pltpu.VMEM((2, ROUNDS) + piece, f32),
            pltpu.VMEM((ROUNDS,) + piece, f32),
            pltpu.VMEM((ROUNDS,) + piece, f32),
            pltpu.VMEM((ROUNDS,) + piece, f32),
            pltpu.VMEM((ROUNDS, 2 * KW, 128), f32),
            pltpu.VMEM((SUBSTEPS, ROUNDS, 2 * KW, 128), f32),
            pltpu.VMEM((SUBSTEPS, ROUNDS, padded, 128), f32),
            pltpu.VMEM((SUBSTEPS, ROUNDS, 2, padded, 128), f32),
            pltpu.VMEM((SUBSTEPS, ROUNDS, 2, 3 * PLANE, 128), f32),
            pltpu.VMEM((SUBSTEPS, ROUNDS, 2, 3 * PLANE, 128), f32),
            dma((ROUNDS, PLANE, 4)),
            dma((ROUNDS, PLANE, 2)),
            dma((SUBSTEPS, ROUNDS, 4)),
            dma((SUBSTEPS, ROUNDS, 2)),
            dma((SUBSTEPS, ROUNDS, 2)),
            dma((ROUNDS, CHIPS)),
            dma((ROUNDS, CHIPS)),
            dma((ROUNDS, PLANE)),
            dma((ROUNDS, PLANE)),
            dma((ROUNDS,)),
            dma((ROUNDS,)),
            dma((ROUNDS, PLANE)),
            dma((ROUNDS, PLANE)),
            dma((ROUNDS, PLANE)),
            dma((ROUNDS, PLANE)),
        ],
        compiler_params=pltpu.CompilerParams(
            collective_id=0, has_side_effects=True, vmem_limit_bytes=60 * 1024 * 1024
        ),
    )(
        jnp.transpose(thickness, (1, 0, 2)),
        jnp.transpose(tracer_mass, (1, 0, 2)),
        jnp.transpose(zonal_courant, (1, 0, 2)),
        jnp.transpose(merid_courant, (1, 0, 2)),
        keep,
        *tables,
    )
    return tuple(jnp.transpose(out, (1, 0, 2)) for out in outs)


def solution(mesh):
    placed = P(None, "lon", "lat")
    return jax.shard_map(
        on_device,
        mesh=mesh,
        in_specs=(placed, placed, placed, placed, P()),
        out_specs=(placed, placed),
        check_vma=False,
    )
```

```python
import functools

import jax
import jax.numpy as jnp
import ml_dtypes
import numpy as np
from jax import lax
from jax.experimental import pallas as pl
from jax.experimental.pallas import tpu as pltpu
from jax.sharding import PartitionSpec as P

KW = 256
SUBSTEPS = 2
PLANE = 8
ROUNDS = 4
CHIPS = PLANE // 2
MESH = pl.DeviceIdType.MESH


def split_table(table):
    high = table.astype(ml_dtypes.bfloat16)
    low = (table - high.astype(np.float64)).astype(ml_dtypes.bfloat16)
    return high, low


def dft_tables(columns, padded, inverse_rows):
    points = columns * PLANE * 2
    longitude = np.arange(PLANE * columns).reshape(PLANE, columns, 1)
    angle = (longitude * np.arange(KW) % points) * (2.0 * np.pi / points)
    table = np.concatenate([np.cos(angle), np.sin(angle)], axis=2)
    forward = np.zeros((PLANE, padded, 2 * KW))
    forward[:, :columns] = table
    inverse = np.zeros((PLANE, inverse_rows, 2 * KW))
    inverse[:, :columns] = table
    forward = forward.reshape(PLANE * padded, 2 * KW).T.copy()
    return split_table(forward) + split_table(inverse.reshape(PLANE * inverse_rows, 2 * KW))


def halves(value):
    high = value.astype(jnp.bfloat16)
    return high, (value - high.astype(jnp.float32)).astype(jnp.bfloat16)


def dot(left, right):
    return jnp.dot(left, right, preferred_element_type=jnp.float32)


def product(left_high, left_low, right):
    right_high, right_low = halves(right)
    return dot(left_high, right_high) + dot(left_high, right_low) + dot(left_low, right_high)


def kernel(
    columns, padded, inverse_rows,
    thick_in, tracer_in, zonal_in, merid_in, keep, fwd_hi_in, fwd_lo_in, inv_hi_in, inv_lo_in,
    thick_out, tracer_out,
    fwd_hi, fwd_lo, inv_hi, inv_lo, table_sem,
    field, zonal, merid, adv, circle, back, passed, spec, spec_in, halo, edge, edge_in, rim, rim_in,
    in_sem, out_sem, halo_send, edge_recv, rim_recv, mig_send, mig_recv, fwd_send, fwd_recv,
    swap_send, swap_recv, ret_send, ret_recv, home_send, home_recv,
):
    band = lax.axis_index("lat")
    lon = lax.axis_index("lon")
    mine = lon % PLANE
    plane = lon - mine
    chip = mine // 2
    across = (lon + PLANE) % (2 * PLANE)
    east = (lon + 1) % (2 * PLANE)
    west = (lon + 2 * PLANE - 1) % (2 * PLANE)
    last_band = band // 7
    first_band = 1 - (band + 7) // 8
    helper_x = (band // 4) * 4 + 3 - band % 4
    helper_z = (band + 4) % 8
    polar = (band < 2) | (band >= 6)
    helping = jnp.logical_not(polar)

    def loop(count, body):
        def run(index, carry):
            body(index)
            return carry

        lax.fori_loop(0, count, run, 0)

    def inner(ref, *place):
        return ref.at[place + (pl.ds(0, columns),)]

    def load_copies(group, level):
        height = group * PLANE + level
        half, slab = level // CHIPS, 2 * (level % CHIPS)
        return [
            pltpu.make_async_copy(thick_in.at[:, height], inner(field, half, group, slab), in_sem.at[group, level, 0]),
            pltpu.make_async_copy(tracer_in.at[:, height], inner(field, half, group, slab + 1), in_sem.at[group, level, 1]),
            pltpu.make_async_copy(zonal_in.at[:, height], inner(zonal, group, level), in_sem.at[group, level, 2]),
            pltpu.make_async_copy(merid_in.at[:, height], inner(merid, group, level), in_sem.at[group, level, 3]),
        ]

    def store_copies(group, level):
        height = group * PLANE + level
        half, slab = level // CHIPS, 2 * (level % CHIPS)
        return [
            pltpu.make_async_copy(inner(field, half, group, slab), thick_out.at[:, height], out_sem.at[group, level, 0]),
            pltpu.make_async_copy(inner(field, half, group, slab + 1), tracer_out.at[:, height], out_sem.at[group, level, 1]),
        ]

    def load(index):
        for copy in load_copies(index // PLANE, index % PLANE):
            copy.start()

    loop(ROUNDS * PLANE, load)
    tables = [
        pltpu.make_async_copy(fwd_hi_in, fwd_hi, table_sem.at[0]),
        pltpu.make_async_copy(fwd_lo_in, fwd_lo, table_sem.at[1]),
        pltpu.make_async_copy(inv_hi_in, inv_hi, table_sem.at[2]),
        pltpu.make_async_copy(inv_lo_in, inv_lo, table_sem.at[3]),
    ]
    for table in tables:
        table.start()

    barrier = pltpu.get_barrier_semaphore()
    partners = [(band, plane + (mine + step) % PLANE) for step in range(1, PLANE)]
    partners += [(band, across), (band, east), (band, west)]
    partners += [((band + 1) % 8, lon), ((band + 7) % 8, lon), (helper_x, lon), (helper_z, across)]
    for partner in partners:
        pl.semaphore_signal(barrier, inc=1, device_id=partner, device_id_type=MESH)

    row = lax.broadcasted_iota(jnp.int32, (padded, 128), 0)
    lane = lax.broadcasted_iota(jnp.int32, (padded, 128), 1)
    rest = pl.ds(columns, padded - columns)
    blank = jnp.zeros((padded - columns, 128), jnp.float32)

    def clear(index):
        group, level = index // PLANE, index % PLANE
        field[0, group, level, rest] = blank
        field[1, group, level, rest] = blank
        zonal[group, level, rest] = blank
        merid[group, level, rest] = blank

    loop(ROUNDS * PLANE, clear)
    pl.semaphore_wait(barrier, len(partners))

    def remote(src, dst, send, recv, device):
        return pltpu.make_async_remote_copy(
            src_ref=src, dst_ref=dst, send_sem=send, recv_sem=recv, device_id=device, device_id_type=MESH
        )

    def halo_copies(step, group):
        return [
            remote(rim.at[step, group, 1], rim_in.at[step, group, 0], halo_send.at[step, group, 0],
                   rim_recv.at[step, group, 0], (band, east)),
            remote(rim.at[step, group, 0], rim_in.at[step, group, 1], halo_send.at[step, group, 1],
                   rim_recv.at[step, group, 1], (band, west)),
            remote(edge.at[step, group, pl.ds(64, 3 * PLANE)], edge_in.at[step, group, last_band], halo_send.at[step, group, 2],
                   edge_recv.at[step, group, last_band],
                   (band + 1 - last_band, (lon + PLANE * last_band) % (2 * PLANE))),
            remote(edge.at[step, group, pl.ds(0, 3 * PLANE)], edge_in.at[step, group, 1 - first_band], halo_send.at[step, group, 3],
                   edge_recv.at[step, group, 1 - first_band],
                   (band - 1 + first_band, (lon + PLANE * first_band) % (2 * PLANE))),
        ]

    def halo_wait(step, group):
        for side in range(2):
            remote(rim.at[step, group, 0], rim_in.at[step, group, side], halo_send.at[step, group, 0],
                   rim_recv.at[step, group, side], (band, east)).wait_recv()
            remote(edge.at[step, group, pl.ds(0, 3 * PLANE)], edge_in.at[step, group, side], halo_send.at[step, group, 0],
                   edge_recv.at[step, group, side], (band, across)).wait_recv()

    def pack(step, group):
        def one(level, packed):
            half, slab = level // CHIPS, 2 * (level % CHIPS)
            values = [field[half, group, slab], field[half, group, slab + 1], merid[group, level]]
            for array, value in enumerate(values):
                place = array * PLANE + level
                packed = jnp.where(lane == place, pltpu.roll(value, place, 1), packed)
                packed = jnp.where(lane == 64 + place, pltpu.roll(value, 65 + place, 1), packed)
            rows = [field.at[half, group, slab], field.at[half, group, slab + 1], zonal.at[group, level]]
            for array, ref in enumerate(rows):
                place = array * PLANE + level
                rim[step, group, 0, pl.ds(place, 1)] = ref[pl.ds(0, 1)]
                rim[step, group, 1, pl.ds(place, 1)] = ref[pl.ds(columns - 1, 1)]
            return packed

        packed = lax.fori_loop(0, PLANE, one, jnp.zeros((padded, 128), jnp.float32))
        edge[step, group] = jnp.transpose(packed)
        for copy in halo_copies(step, group):
            copy.start()

    sign_south = 1.0 - 2.0 * first_band.astype(jnp.float32)
    sign_north = 1.0 - 2.0 * last_band.astype(jnp.float32)

    def advect(step, group, level):
        half, slab = level // CHIPS, 2 * (level % CHIPS)

        def eastward(value, rim_row):
            return jnp.where(row == columns - 1, rim_row, pltpu.roll(value, padded - 1, 0))

        def rims(place):
            return rim_in[step, group, 0, pl.ds(place, 1)], rim_in[step, group, 1, pl.ds(place, 1)]

        def northward(place, value, sign):
            column = pltpu.roll(halo[1], 127 - place, 1)
            return jnp.where(lane == 127, column if sign is None else sign * column, pltpu.roll(value, 127, 1))

        def southward(place, value, sign):
            column = pltpu.roll(halo[0], 128 - place, 1)
            return jnp.where(lane == 0, column if sign is None else sign * column, pltpu.roll(value, 1, 1))

        a = zonal[group, level]
        m = merid[group, level]
        west_a, east_a = rims(2 * PLANE + level)
        face_east = 0.5 * (a + eastward(a, east_a))
        face_west = 0.5 * (west_a + a[0:1])
        face_north = 0.5 * (m + northward(2 * PLANE + level, m, sign_north))
        face_south = 0.5 * (southward(2 * PLANE + level, m, sign_south) + m)
        results = []
        for array in range(2):
            f = field[half, group, slab + array]
            place = array * PLANE + level
            west_f, east_f = rims(place)
            flux_east = jnp.maximum(face_east, 0.0) * f + jnp.minimum(face_east, 0.0) * eastward(f, east_f)
            first_west = jnp.maximum(face_west, 0.0) * west_f + jnp.minimum(face_west, 0.0) * f[0:1]
            flux_west = jnp.where(row == 0, first_west, pltpu.roll(flux_east, 1, 0))
            flux_north = jnp.maximum(face_north, 0.0) * f + jnp.minimum(face_north, 0.0) * northward(place, f, None)
            flux_south = jnp.maximum(face_south, 0.0) * southward(place, f, None) + jnp.minimum(face_south, 0.0) * f
            result = f - (flux_east - flux_west) - (flux_north - flux_south)
            results.append(jnp.where(row < columns, result, 0.0))
        return results


    def mig_copy(unit, place, device):
        pair = pl.ds(2 * place, 2)
        return remote(adv.at[1, unit, pair], adv.at[0, unit, pair], mig_send.at[unit, place], mig_recv.at[unit, place],
                      device)

    def fwd_copy(unit, slab):
        return remote(adv.at[0, unit, slab], circle.at[unit, mine], fwd_send.at[unit, slab], fwd_recv.at[unit, mine],
                      (band, plane + slab))

    def own_copy(unit):
        return pltpu.make_async_copy(adv.at[0, unit, mine], circle.at[unit, mine], fwd_send.at[unit, mine])

    def swap_copy(step, unit):
        return remote(spec.at[unit], spec_in.at[step, unit], swap_send.at[unit], swap_recv.at[unit], (band, across))

    def ret_copy(unit, other, target):
        return remote(back.at[unit, other], target.at[unit, mine], ret_send.at[unit, other], ret_recv.at[unit, mine],
                      (band, plane + other))

    def home_copy(unit, slab, device):
        return remote(passed.at[unit, slab], field.at[1, unit, slab], home_send.at[unit, slab], home_recv.at[unit, slab],
                      device)

    def send_forward(unit, slab):
        @pl.when(slab != mine)
        def _():
            fwd_copy(unit, slab).start()

        @pl.when(slab == mine)
        def _():
            own_copy(unit).start()

    def given(unit):
        def one(index):
            ret_copy(unit, (mine + 1 + index) % PLANE, passed).wait_send()

        loop(PLANE - 1, one)

    def handed(unit):
        def one(slab):
            home_copy(unit, slab, (helper_x, lon)).wait_send()

        given(unit)
        loop(PLANE, one)

    def prepare(item):
        step, unit = item // ROUNDS, item % ROUNDS

        @pl.when(step == 0)
        def _():
            def loaded(level):
                for copy in load_copies(unit, level):
                    copy.wait()

            loop(PLANE, loaded)

        @pl.when((step > 0) & polar)
        def _():
            def landed(index):
                source = (mine + PLANE - 1 - index) % PLANE
                remote(back.at[unit, source], field.at[0, unit, source], ret_send.at[unit, source],
                       ret_recv.at[unit, source], (band, plane + source)).wait_recv()

            def sent(place):
                mig_copy(unit, place, (helper_x, lon)).wait_send()

            def home(slab):
                home_copy(unit, slab, (helper_x, lon)).wait_recv()

            given(unit)
            loop(PLANE - 1, landed)
            loop(CHIPS, sent)
            loop(PLANE, home)

        @pl.when(step < SUBSTEPS)
        def _():
            pack(step, unit)

        @pl.when(step == SUBSTEPS)
        def _():
            def store(level):
                for copy in store_copies(unit, level):
                    copy.start()

            loop(PLANE, store)

    def advance(item):
        step, unit = item // ROUNDS, item % ROUNDS
        halo_wait(step, unit)
        unused = jnp.zeros((128 - 3 * PLANE, padded), jnp.float32)
        for side in range(2):
            halo[side] = jnp.transpose(jnp.concatenate([edge_in[step, unit, side], unused], axis=0))

        def one(index):
            half = 1 - index % 2
            place = (chip + 1 + index // 2) % CHIPS
            slab = 2 * place
            first, second = advect(step, unit, half * CHIPS + place)

            @pl.when(helping)
            def _():
                field[half, unit, slab] = first
                field[half, unit, slab + 1] = second

            @pl.when(polar)
            def _():
                adv[half, unit, slab] = first
                adv[half, unit, slab + 1] = second

                @pl.when((half == 1) & (place < CHIPS // 2))
                def _():
                    mig_copy(unit, place, (helper_x, lon)).start()

                @pl.when((half == 1) & (place >= CHIPS // 2))
                def _():
                    mig_copy(unit, place, (helper_z, across)).start()

                @pl.when(half == 0)
                def _():
                    send_forward(unit, slab)
                    send_forward(unit, slab + 1)

        loop(PLANE, one)

    def relay(item):
        unit = item % ROUNDS

        @pl.when(item >= ROUNDS)
        def _():
            handed(unit)

        def one(index):
            place = (chip + 1 + index) % CHIPS
            mig_copy(unit, place, (helper_x, lon)).wait_recv()
            send_forward(unit, 2 * place)
            send_forward(unit, 2 * place + 1)

        loop(CHIPS, one)

    def transform(item):
        step, unit = item // ROUNDS, item % ROUNDS
        @pl.when(item == 0)
        def _():
            for table in tables:
                table.wait()

        own_copy(unit).wait()

        def arrived(index):
            source = (mine + PLANE - 1 - index) % PLANE
            remote(adv.at[0, unit, source], circle.at[unit, source], fwd_send.at[unit, source],
                   fwd_recv.at[unit, source], (band, plane + source)).wait_recv()

        loop(PLANE - 1, arrived)
        spec[unit] = product(fwd_hi[...], fwd_lo[...], circle[unit].reshape(PLANE * padded, 128))
        swap_copy(step, unit).start()

    wave_row = lax.broadcasted_iota(jnp.int32, (2 * KW, 128), 0)
    parity = 1.0 - 2.0 * (wave_row % 2).astype(jnp.float32)

    def restore(item):
        step, unit = item // ROUNDS, item % ROUNDS

        def sent(index):
            fwd_copy(unit, (mine + 1 + index) % PLANE).wait_send()

        loop(PLANE - 1, sent)
        swap_copy(step, unit).wait()
        kept_hi, kept_lo = halves((spec[unit] + parity * spec_in[step, unit]) * keep[mine // CHIPS])

        def give(index):
            other = (mine + 1 + index) % PLANE
            place = pl.ds(pl.multiple_of(other * inverse_rows, inverse_rows), inverse_rows)
            value = dot(inv_hi[place], kept_hi) + dot(inv_hi[place], kept_lo) + dot(inv_lo[place], kept_hi)
            value = value[:padded]

            @pl.when(other != mine)
            def _():
                back[unit, other] = value

            @pl.when((other != mine) & polar)
            def _():
                ret_copy(unit, other, field.at[0]).start()

            @pl.when((other != mine) & helping)
            def _():
                ret_copy(unit, other, passed).start()

            @pl.when((other == mine) & polar)
            def _():
                field[0, unit, mine] = value

            @pl.when((other == mine) & helping)
            def _():
                passed[unit, mine] = value

        loop(PLANE, give)

    def send_home(item):
        unit = item % ROUNDS

        def one(index):
            slab = (mine + PLANE - index) % PLANE

            @pl.when(slab != mine)
            def _():
                remote(back.at[unit, slab], passed.at[unit, slab], ret_send.at[unit, slab],
                       ret_recv.at[unit, slab], (band, plane + slab)).wait_recv()

            @pl.when(slab < CHIPS)
            def _():
                home_copy(unit, slab, (helper_x, lon)).start()

            @pl.when(slab >= CHIPS)
            def _():
                home_copy(unit, slab, (helper_z, across)).start()

        loop(PLANE, one)

    items = SUBSTEPS * ROUNDS

    def tick(time):
        @pl.when((time < items) & polar)
        def _():
            advance(time)

        @pl.when((time + 2 < ROUNDS) & polar)
        def _():
            prepare(time + 2)

        @pl.when((time + 1 >= ROUNDS) & polar)
        def _():
            prepare(time + 1)

        @pl.when((time >= 3) & helping)
        def _():
            send_home(time - 3)

        @pl.when((time >= 2) & (time < items + 2))
        def _():
            restore(time - 2)

        @pl.when((time >= 1) & (time < items + 1))
        def _():
            transform(time - 1)

        @pl.when((time < items) & helping)
        def _():
            relay(time)
            advance(time)

        @pl.when((time < items) & helping)
        def _():
            prepare(time + ROUNDS)

    @pl.when(polar)
    def _():
        loop(2, prepare)

    @pl.when(helping)
    def _():
        loop(ROUNDS, prepare)

    loop(items + 3, tick)

    @pl.when(helping)
    def _():
        loop(ROUNDS, handed)

    def halo_done(index):
        for copy in halo_copies(index // ROUNDS, index % ROUNDS):
            copy.wait_send()

    loop(items, halo_done)

    def stored(index):
        for copy in store_copies(index // PLANE, index % PLANE):
            copy.wait()

    loop(ROUNDS * PLANE, stored)


def kept_waves(cutoffs, source_band, lat_rows, points):
    quarter_rows = cutoffs.shape[0] // 2
    latitude = source_band * lat_rows + jnp.arange(lat_rows, dtype=jnp.int32)
    polar_index = jnp.where(latitude < quarter_rows, latitude, latitude - 2 * quarter_rows)
    slots = jnp.arange(cutoffs.shape[0], dtype=jnp.int32)
    row_cut = jnp.sum(jnp.where(polar_index[:, None] == slots[None, :], cutoffs[None, :], 0), axis=1)
    wave = jnp.arange(KW, dtype=jnp.int32)
    weight = (jnp.where(wave == 0, 1.0, 2.0) / points).astype(jnp.float32)
    kept = jnp.where(wave[:, None] < row_cut[None, :], weight[:, None], 0.0)
    return jnp.concatenate([kept, kept], axis=0)


def on_device(thickness, tracer_mass, zonal_courant, merid_courant, cutoffs):
    band = lax.axis_index("lat")
    levels, columns, lat_rows = thickness.shape
    points = columns * lax.axis_size("lon")
    padded = -(-columns // 8) * 8
    inverse_rows = -(-columns // 16) * 16
    polar = (band < 2) | (band >= 6)
    helped_x = (band // 4) * 4 + 3 - band % 4
    helped_z = (band + 4) % 8
    keep = jnp.stack(
        [
            kept_waves(cutoffs, jnp.where(polar, band, helped_x), lat_rows, points),
            kept_waves(cutoffs, jnp.where(polar, band, helped_z), lat_rows, points),
        ]
    )
    tables = [jnp.asarray(table) for table in dft_tables(columns, padded, inverse_rows)]
    shape = (columns, levels, lat_rows)
    f32 = jnp.float32
    dma = pltpu.SemaphoreType.DMA
    piece = (PLANE, padded, 128)
    outs = pl.pallas_call(
        functools.partial(kernel, columns, padded, inverse_rows),
        out_shape=[jax.ShapeDtypeStruct(shape, f32)] * 2,
        in_specs=[pl.BlockSpec(memory_space=pl.ANY)] * 4
        + [pl.BlockSpec(memory_space=pltpu.VMEM)]
        + [pl.BlockSpec(memory_space=pl.ANY)] * 4,
        out_specs=[pl.BlockSpec(memory_space=pl.ANY)] * 2,
        scratch_shapes=[pltpu.VMEM(table.shape, table.dtype) for table in tables]
        + [
            dma((4,)),
            pltpu.VMEM((2, ROUNDS) + piece, f32),
            pltpu.VMEM((ROUNDS,) + piece, f32),
            pltpu.VMEM((ROUNDS,) + piece, f32),
            pltpu.VMEM((2, ROUNDS) + piece, f32),
            pltpu.VMEM((ROUNDS,) + piece, f32),
            pltpu.VMEM((ROUNDS,) + piece, f32),
            pltpu.VMEM((ROUNDS,) + piece, f32),
            pltpu.VMEM((ROUNDS, 2 * KW, 128), f32),
            pltpu.VMEM((SUBSTEPS, ROUNDS, 2 * KW, 128), f32),
            pltpu.VMEM((2, padded, 128), f32),
            pltpu.VMEM((SUBSTEPS, ROUNDS, 128, padded), f32),
            pltpu.VMEM((SUBSTEPS, ROUNDS, 2, 3 * PLANE, padded), f32),
            pltpu.VMEM((SUBSTEPS, ROUNDS, 2, 3 * PLANE, 128), f32),
            pltpu.VMEM((SUBSTEPS, ROUNDS, 2, 3 * PLANE, 128), f32),
            dma((ROUNDS, PLANE, 4)),
            dma((ROUNDS, PLANE, 2)),
            dma((SUBSTEPS, ROUNDS, 4)),
            dma((SUBSTEPS, ROUNDS, 2)),
            dma((SUBSTEPS, ROUNDS, 2)),
            dma((ROUNDS, CHIPS)),
            dma((ROUNDS, CHIPS)),
            dma((ROUNDS, PLANE)),
            dma((ROUNDS, PLANE)),
            dma((ROUNDS,)),
            dma((ROUNDS,)),
            dma((ROUNDS, PLANE)),
            dma((ROUNDS, PLANE)),
            dma((ROUNDS, PLANE)),
            dma((ROUNDS, PLANE)),
        ],
        compiler_params=pltpu.CompilerParams(
            collective_id=0, has_side_effects=True, vmem_limit_bytes=60 * 1024 * 1024
        ),
    )(
        jnp.transpose(thickness, (1, 0, 2)),
        jnp.transpose(tracer_mass, (1, 0, 2)),
        jnp.transpose(zonal_courant, (1, 0, 2)),
        jnp.transpose(merid_courant, (1, 0, 2)),
        keep,
        *tables,
    )
    return tuple(jnp.transpose(out, (1, 0, 2)) for out in outs)


def solution(mesh):
    placed = P(None, "lon", "lat")
    return jax.shard_map(
        on_device,
        mesh=mesh,
        in_specs=(placed, placed, placed, placed, P()),
        out_specs=(placed, placed),
        check_vma=False,
    )
```

```python
import functools

import jax
import jax.numpy as jnp
import ml_dtypes
import numpy as np
from jax import lax
from jax.experimental import pallas as pl
from jax.experimental.pallas import tpu as pltpu
from jax.sharding import PartitionSpec as P

KW = 256
SUBSTEPS = 2
PLANE = 8
ROUNDS = 4
CHIPS = PLANE // 2
MESH = pl.DeviceIdType.MESH


def split_table(table):
    high = table.astype(ml_dtypes.bfloat16)
    low = (table - high.astype(np.float64)).astype(ml_dtypes.bfloat16)
    return high, low


def dft_tables(columns, padded, inverse_rows):
    points = columns * PLANE * 2
    longitude = np.arange(PLANE * columns).reshape(PLANE, columns, 1)
    angle = (longitude * np.arange(KW) % points) * (2.0 * np.pi / points)
    table = np.concatenate([np.cos(angle), np.sin(angle)], axis=2)
    forward = np.zeros((PLANE, padded, 2 * KW))
    forward[:, :columns] = table
    inverse = np.zeros((PLANE, inverse_rows, 2 * KW))
    inverse[:, :columns] = table
    forward = forward.reshape(PLANE * padded, 2 * KW).T.copy()
    return split_table(forward) + split_table(inverse.reshape(PLANE * inverse_rows, 2 * KW))


def halves(value):
    high = value.astype(jnp.bfloat16)
    return high, (value - high.astype(jnp.float32)).astype(jnp.bfloat16)


def dot(left, right):
    return jnp.dot(left, right, preferred_element_type=jnp.float32)


def product(left_high, left_low, right):
    right_high, right_low = halves(right)
    return dot(left_high, right_high) + dot(left_high, right_low) + dot(left_low, right_high)


def kernel(
    columns, padded, inverse_rows,
    thick_in, tracer_in, zonal_in, merid_in, cuts, fwd_hi_in, fwd_lo_in, inv_hi_in, inv_lo_in,
    thick_out, tracer_out,
    fwd_hi, fwd_lo, inv_hi, inv_lo, table_sem,
    field, zonal, merid, adv, circle, back, passed, spec, spec_in, halo, edge, edge_in, rim, rim_in,
    in_sem, out_sem, halo_send, edge_recv, rim_recv, mig_send, mig_recv, fwd_send, fwd_recv,
    swap_send, swap_recv, ret_send, ret_recv, home_send, home_recv,
):
    band = lax.axis_index("lat")
    lon = lax.axis_index("lon")
    mine = lon % PLANE
    plane = lon - mine
    chip = mine // 2
    across = (lon + PLANE) % (2 * PLANE)
    east = (lon + 1) % (2 * PLANE)
    west = (lon + 2 * PLANE - 1) % (2 * PLANE)
    last_band = band // 7
    first_band = 1 - (band + 7) // 8
    helper_x = (band // 4) * 4 + 3 - band % 4
    helper_z = (band + 4) % 8
    polar = (band < 2) | (band >= 6)
    helping = jnp.logical_not(polar)

    def loop(count, body):
        def run(index, carry):
            body(index)
            return carry

        lax.fori_loop(0, count, run, 0)

    def inner(ref, *place):
        return ref.at[place + (pl.ds(0, columns),)]

    def load_copies(group, level):
        height = group * PLANE + level
        half, slab = level // CHIPS, 2 * (level % CHIPS)
        return [
            pltpu.make_async_copy(thick_in.at[:, height], inner(field, half, group, slab), in_sem.at[group, level, 0]),
            pltpu.make_async_copy(tracer_in.at[:, height], inner(field, half, group, slab + 1), in_sem.at[group, level, 1]),
            pltpu.make_async_copy(zonal_in.at[:, height], inner(zonal, group, level), in_sem.at[group, level, 2]),
            pltpu.make_async_copy(merid_in.at[:, height], inner(merid, group, level), in_sem.at[group, level, 3]),
        ]

    def store_copies(group, level):
        height = group * PLANE + level
        half, slab = level // CHIPS, 2 * (level % CHIPS)
        return [
            pltpu.make_async_copy(inner(field, half, group, slab), thick_out.at[:, height], out_sem.at[group, level, 0]),
            pltpu.make_async_copy(inner(field, half, group, slab + 1), tracer_out.at[:, height], out_sem.at[group, level, 1]),
        ]

    def load(index):
        for copy in load_copies(index // PLANE, index % PLANE):
            copy.start()

    loop(ROUNDS * PLANE, load)
    tables = [
        pltpu.make_async_copy(fwd_hi_in, fwd_hi, table_sem.at[0]),
        pltpu.make_async_copy(fwd_lo_in, fwd_lo, table_sem.at[1]),
        pltpu.make_async_copy(inv_hi_in, inv_hi, table_sem.at[2]),
        pltpu.make_async_copy(inv_lo_in, inv_lo, table_sem.at[3]),
    ]
    for table in tables:
        table.start()

    barrier = pltpu.get_barrier_semaphore()
    partners = [(band, plane + (mine + step) % PLANE) for step in range(1, PLANE)]
    partners += [(band, across), (band, east), (band, west)]
    partners += [((band + 1) % 8, lon), ((band + 7) % 8, lon), (helper_x, lon), (helper_z, across)]
    for partner in partners:
        pl.semaphore_signal(barrier, inc=1, device_id=partner, device_id_type=MESH)

    row = lax.broadcasted_iota(jnp.int32, (padded, 128), 0)
    lane = lax.broadcasted_iota(jnp.int32, (padded, 128), 1)
    rest = pl.ds(columns, padded - columns)
    blank = jnp.zeros((padded - columns, 128), jnp.float32)

    def clear(index):
        group, level = index // PLANE, index % PLANE
        field[0, group, level, rest] = blank
        field[1, group, level, rest] = blank
        zonal[group, level, rest] = blank
        circle[group, level, rest] = blank
        merid[group, level, rest] = blank

    loop(ROUNDS * PLANE, clear)
    pl.semaphore_wait(barrier, len(partners))

    def remote(src, dst, send, recv, device):
        return pltpu.make_async_remote_copy(
            src_ref=src, dst_ref=dst, send_sem=send, recv_sem=recv, device_id=device, device_id_type=MESH
        )

    def halo_copies(step, group):
        return [
            remote(rim.at[step, group, 1], rim_in.at[step, group, 0], halo_send.at[step, group, 0],
                   rim_recv.at[step, group, 0], (band, east)),
            remote(rim.at[step, group, 0], rim_in.at[step, group, 1], halo_send.at[step, group, 1],
                   rim_recv.at[step, group, 1], (band, west)),
            remote(edge.at[step, group, pl.ds(64, 3 * PLANE)], edge_in.at[step, group, last_band], halo_send.at[step, group, 2],
                   edge_recv.at[step, group, last_band],
                   (band + 1 - last_band, (lon + PLANE * last_band) % (2 * PLANE))),
            remote(edge.at[step, group, pl.ds(0, 3 * PLANE)], edge_in.at[step, group, 1 - first_band], halo_send.at[step, group, 3],
                   edge_recv.at[step, group, 1 - first_band],
                   (band - 1 + first_band, (lon + PLANE * first_band) % (2 * PLANE))),
        ]

    def halo_wait(step, group):
        for side in range(2):
            remote(rim.at[step, group, 0], rim_in.at[step, group, side], halo_send.at[step, group, 0],
                   rim_recv.at[step, group, side], (band, east)).wait_recv()
            remote(edge.at[step, group, pl.ds(0, 3 * PLANE)], edge_in.at[step, group, side], halo_send.at[step, group, 0],
                   edge_recv.at[step, group, side], (band, across)).wait_recv()

    def pack(step, group):
        def one(level, packed):
            half, slab = level // CHIPS, 2 * (level % CHIPS)
            values = [field[half, group, slab], field[half, group, slab + 1], merid[group, level]]
            for array, value in enumerate(values):
                place = array * PLANE + level
                packed = jnp.where(lane == place, pltpu.roll(value, place, 1), packed)
                packed = jnp.where(lane == 64 + place, pltpu.roll(value, 65 + place, 1), packed)
            outer = [field.at[half, group, slab], field.at[half, group, slab + 1], zonal.at[group, level]]
            for array, ref in enumerate(outer):
                place = array * PLANE + level
                rim[step, group, 0, pl.ds(place, 1)] = ref[pl.ds(0, 1)]
                rim[step, group, 1, pl.ds(place, 1)] = ref[pl.ds(columns - 1, 1)]
            return packed

        packed = lax.fori_loop(0, PLANE, one, jnp.zeros((padded, 128), jnp.float32))
        edge[step, group] = jnp.transpose(packed)
        for copy in halo_copies(step, group):
            copy.start()

    sign_south = 1.0 - 2.0 * first_band.astype(jnp.float32)
    sign_north = 1.0 - 2.0 * last_band.astype(jnp.float32)

    def advect(step, group, level):
        half, slab = level // CHIPS, 2 * (level % CHIPS)

        def eastward(value, rim_row):
            return jnp.where(row == columns - 1, rim_row, pltpu.roll(value, padded - 1, 0))

        def rims(place):
            return rim_in[step, group, 0, pl.ds(place, 1)], rim_in[step, group, 1, pl.ds(place, 1)]

        def northward(place, value, sign):
            column = pltpu.roll(halo[1], 127 - place, 1)
            return jnp.where(lane == 127, column if sign is None else sign * column, pltpu.roll(value, 127, 1))

        def southward(place, value, sign):
            column = pltpu.roll(halo[0], 128 - place, 1)
            return jnp.where(lane == 0, column if sign is None else sign * column, pltpu.roll(value, 1, 1))

        a = zonal[group, level]
        m = merid[group, level]
        west_a, east_a = rims(2 * PLANE + level)
        face_east = 0.5 * (a + eastward(a, east_a))
        face_west = 0.5 * (west_a + a[0:1])
        face_north = 0.5 * (m + northward(2 * PLANE + level, m, sign_north))
        face_south = 0.5 * (southward(2 * PLANE + level, m, sign_south) + m)
        results = []
        for array in range(2):
            f = field[half, group, slab + array]
            place = array * PLANE + level
            west_f, east_f = rims(place)
            flux_east = jnp.maximum(face_east, 0.0) * f + jnp.minimum(face_east, 0.0) * eastward(f, east_f)
            first_west = jnp.maximum(face_west, 0.0) * west_f + jnp.minimum(face_west, 0.0) * f[0:1]
            flux_west = jnp.where(row == 0, first_west, pltpu.roll(flux_east, 1, 0))
            flux_north = jnp.maximum(face_north, 0.0) * f + jnp.minimum(face_north, 0.0) * northward(place, f, None)
            flux_south = jnp.maximum(face_south, 0.0) * southward(place, f, None) + jnp.minimum(face_south, 0.0) * f
            result = f - (flux_east - flux_west) - (flux_north - flux_south)
            results.append(jnp.where(row < columns, result, 0.0))
        return results


    rows = pl.ds(0, columns)

    def mig_copy(unit, place, device):
        pair = pl.ds(2 * place, 2)
        return remote(adv.at[1, unit, pair, rows], adv.at[0, unit, pair, rows], mig_send.at[unit, place], mig_recv.at[unit, place],
                      device)

    def fwd_copy(unit, slab):
        return remote(adv.at[0, unit, slab, rows], circle.at[unit, mine, rows], fwd_send.at[unit, slab], fwd_recv.at[unit, mine],
                      (band, plane + slab))

    def own_copy(unit):
        return pltpu.make_async_copy(adv.at[0, unit, mine, rows], circle.at[unit, mine, rows], fwd_send.at[unit, mine])

    def swap_copy(step, unit):
        return remote(spec.at[unit], spec_in.at[step, unit], swap_send.at[unit], swap_recv.at[unit], (band, across))

    def ret_copy(unit, other, target):
        return remote(back.at[unit, other, rows], target.at[unit, mine, rows], ret_send.at[unit, other], ret_recv.at[unit, mine],
                      (band, plane + other))

    def home_copy(unit, slab, device):
        return remote(passed.at[unit, slab, rows], field.at[1, unit, slab, rows], home_send.at[unit, slab], home_recv.at[unit, slab],
                      device)

    def send_forward(unit, slab):
        @pl.when(slab != mine)
        def _():
            fwd_copy(unit, slab).start()

        @pl.when(slab == mine)
        def _():
            own_copy(unit).start()

    def given(unit):
        def one(index):
            ret_copy(unit, (mine + 1 + index) % PLANE, passed).wait_send()

        loop(PLANE - 1, one)

    def handed(unit):
        def one(slab):
            home_copy(unit, slab, (helper_x, lon)).wait_send()

        given(unit)
        loop(PLANE, one)

    def prepare(item):
        step, unit = item // ROUNDS, item % ROUNDS

        @pl.when(step == 0)
        def _():
            def loaded(level):
                for copy in load_copies(unit, level):
                    copy.wait()

            loop(PLANE, loaded)

        @pl.when((step > 0) & polar)
        def _():
            def landed(index):
                source = (mine + PLANE - 1 - index) % PLANE
                remote(back.at[unit, source, rows], field.at[0, unit, source, rows], ret_send.at[unit, source],
                       ret_recv.at[unit, source], (band, plane + source)).wait_recv()

            def sent(place):
                mig_copy(unit, place, (helper_x, lon)).wait_send()

            def home(slab):
                home_copy(unit, slab, (helper_x, lon)).wait_recv()

            given(unit)
            loop(PLANE - 1, landed)
            loop(CHIPS, sent)
            loop(PLANE, home)

        @pl.when(step < SUBSTEPS)
        def _():
            pack(step, unit)

        @pl.when(step == SUBSTEPS)
        def _():
            def store(level):
                for copy in store_copies(unit, level):
                    copy.start()

            loop(PLANE, store)

    def advance(item):
        step, unit = item // ROUNDS, item % ROUNDS
        halo_wait(step, unit)
        unused = jnp.zeros((128 - 3 * PLANE, padded), jnp.float32)
        for side in range(2):
            halo[side] = jnp.transpose(jnp.concatenate([edge_in[step, unit, side], unused], axis=0))

        def one(index):
            half = 1 - index % 2
            place = (chip + 1 + index // 2) % CHIPS
            slab = 2 * place
            first, second = advect(step, unit, half * CHIPS + place)

            @pl.when(helping)
            def _():
                field[half, unit, slab] = first
                field[half, unit, slab + 1] = second

            @pl.when(polar)
            def _():
                adv[half, unit, slab] = first
                adv[half, unit, slab + 1] = second

                @pl.when((half == 1) & (place < CHIPS // 2))
                def _():
                    mig_copy(unit, place, (helper_x, lon)).start()

                @pl.when((half == 1) & (place >= CHIPS // 2))
                def _():
                    mig_copy(unit, place, (helper_z, across)).start()

                @pl.when(half == 0)
                def _():
                    send_forward(unit, slab)
                    send_forward(unit, slab + 1)

        loop(PLANE, one)

    def relay(item):
        unit = item % ROUNDS

        @pl.when(item >= ROUNDS)
        def _():
            handed(unit)

        def one(index):
            place = (chip + 1 + index) % CHIPS
            mig_copy(unit, place, (helper_x, lon)).wait_recv()
            send_forward(unit, 2 * place)
            send_forward(unit, 2 * place + 1)

        loop(CHIPS, one)

    def transform(item):
        step, unit = item // ROUNDS, item % ROUNDS
        @pl.when(item == 0)
        def _():
            for table in tables:
                table.wait()

        own_copy(unit).wait()

        def arrived(index):
            source = (mine + PLANE - 1 - index) % PLANE
            remote(adv.at[0, unit, source, rows], circle.at[unit, source, rows], fwd_send.at[unit, source],
                   fwd_recv.at[unit, source], (band, plane + source)).wait_recv()

        loop(PLANE - 1, arrived)
        spec[unit] = product(fwd_hi[...], fwd_lo[...], circle[unit].reshape(PLANE * padded, 128))
        swap_copy(step, unit).start()

    wave_row = lax.broadcasted_iota(jnp.int32, (2 * KW, 128), 0)
    parity = 1.0 - 2.0 * (wave_row % 2).astype(jnp.float32)
    wave = wave_row % KW
    wave_weight = jnp.where(wave == 0, 1.0 / (2 * PLANE * columns), 2.0 / (2 * PLANE * columns))
    source_band = jnp.where(polar, band, jnp.where(mine < CHIPS, helper_x, helper_z))

    def restore(item):
        step, unit = item // ROUNDS, item % ROUNDS

        def sent(index):
            fwd_copy(unit, (mine + 1 + index) % PLANE).wait_send()

        loop(PLANE - 1, sent)
        swap_copy(step, unit).wait()
        kept = jnp.where(wave < cuts[pl.ds(source_band % 4, 1)], wave_weight, 0.0)
        kept_hi, kept_lo = halves((spec[unit] + parity * spec_in[step, unit]) * kept)

        def give(index):
            other = (mine + 1 + index) % PLANE
            place = pl.ds(pl.multiple_of(other * inverse_rows, inverse_rows), inverse_rows)
            value = dot(inv_hi[place], kept_hi) + dot(inv_hi[place], kept_lo) + dot(inv_lo[place], kept_hi)
            value = value[:padded]

            @pl.when(other != mine)
            def _():
                back[unit, other] = value

            @pl.when((other != mine) & polar)
            def _():
                ret_copy(unit, other, field.at[0]).start()

            @pl.when((other != mine) & helping)
            def _():
                ret_copy(unit, other, passed).start()

            @pl.when((other == mine) & polar)
            def _():
                field[0, unit, mine] = value

            @pl.when((other == mine) & helping)
            def _():
                passed[unit, mine] = value

        loop(PLANE, give)

    def send_home(item):
        unit = item % ROUNDS

        def one(index):
            slab = (mine + PLANE - index) % PLANE

            @pl.when(slab != mine)
            def _():
                remote(back.at[unit, slab, rows], passed.at[unit, slab, rows], ret_send.at[unit, slab],
                       ret_recv.at[unit, slab], (band, plane + slab)).wait_recv()

            @pl.when(slab < CHIPS)
            def _():
                home_copy(unit, slab, (helper_x, lon)).start()

            @pl.when(slab >= CHIPS)
            def _():
                home_copy(unit, slab, (helper_z, across)).start()

        loop(PLANE, one)

    items = SUBSTEPS * ROUNDS

    def tick(time):
        @pl.when((time < items) & polar)
        def _():
            advance(time)

        @pl.when((time + 2 < ROUNDS) & polar)
        def _():
            prepare(time + 2)

        @pl.when((time + 1 >= ROUNDS) & (time < items) & polar)
        def _():
            prepare(time + 1)

        @pl.when((time >= 3) & helping)
        def _():
            send_home(time - 3)

        @pl.when((time >= 2) & (time < items + 2))
        def _():
            restore(time - 2)

        @pl.when((time >= 1) & (time < items + 1))
        def _():
            transform(time - 1)

        @pl.when((time >= items) & polar)
        def _():
            prepare(time + 1)

        @pl.when((time < items) & helping)
        def _():
            relay(time)
            advance(time)

        @pl.when((time < items) & helping)
        def _():
            prepare(time + ROUNDS)

    @pl.when(polar)
    def _():
        loop(2, prepare)

    @pl.when(helping)
    def _():
        loop(ROUNDS, prepare)

    loop(items + 3, tick)

    @pl.when(helping)
    def _():
        loop(ROUNDS, handed)

    def halo_done(index):
        for copy in halo_copies(index // ROUNDS, index % ROUNDS):
            copy.wait_send()

    loop(items, halo_done)

    def stored(index):
        for copy in store_copies(index // PLANE, index % PLANE):
            copy.wait()

    loop(ROUNDS * PLANE, stored)


def on_device(thickness, tracer_mass, zonal_courant, merid_courant, cutoffs):
    levels, columns, lat_rows = thickness.shape
    padded = -(-columns // 8) * 8
    inverse_rows = -(-columns // 16) * 16
    tables = [jnp.asarray(table) for table in dft_tables(columns, padded, inverse_rows)]
    shape = (columns, levels, lat_rows)
    f32 = jnp.float32
    dma = pltpu.SemaphoreType.DMA
    piece = (PLANE, padded, 128)
    outs = pl.pallas_call(
        functools.partial(kernel, columns, padded, inverse_rows),
        out_shape=[jax.ShapeDtypeStruct(shape, f32)] * 2,
        in_specs=[pl.BlockSpec(memory_space=pl.ANY)] * 4
        + [pl.BlockSpec(memory_space=pltpu.VMEM)]
        + [pl.BlockSpec(memory_space=pl.ANY)] * 4,
        out_specs=[pl.BlockSpec(memory_space=pl.ANY)] * 2,
        scratch_shapes=[pltpu.VMEM(table.shape, table.dtype) for table in tables]
        + [
            dma((4,)),
            pltpu.VMEM((2, ROUNDS) + piece, f32),
            pltpu.VMEM((ROUNDS,) + piece, f32),
            pltpu.VMEM((ROUNDS,) + piece, f32),
            pltpu.VMEM((2, ROUNDS) + piece, f32),
            pltpu.VMEM((ROUNDS,) + piece, f32),
            pltpu.VMEM((ROUNDS,) + piece, f32),
            pltpu.VMEM((ROUNDS,) + piece, f32),
            pltpu.VMEM((ROUNDS, 2 * KW, 128), f32),
            pltpu.VMEM((SUBSTEPS, ROUNDS, 2 * KW, 128), f32),
            pltpu.VMEM((2, padded, 128), f32),
            pltpu.VMEM((SUBSTEPS, ROUNDS, 128, padded), f32),
            pltpu.VMEM((SUBSTEPS, ROUNDS, 2, 3 * PLANE, padded), f32),
            pltpu.VMEM((SUBSTEPS, ROUNDS, 2, 3 * PLANE, 128), f32),
            pltpu.VMEM((SUBSTEPS, ROUNDS, 2, 3 * PLANE, 128), f32),
            dma((ROUNDS, PLANE, 4)),
            dma((ROUNDS, PLANE, 2)),
            dma((SUBSTEPS, ROUNDS, 4)),
            dma((SUBSTEPS, ROUNDS, 2)),
            dma((SUBSTEPS, ROUNDS, 2)),
            dma((ROUNDS, CHIPS)),
            dma((ROUNDS, CHIPS)),
            dma((ROUNDS, PLANE)),
            dma((ROUNDS, PLANE)),
            dma((ROUNDS,)),
            dma((ROUNDS,)),
            dma((ROUNDS, PLANE)),
            dma((ROUNDS, PLANE)),
            dma((ROUNDS, PLANE)),
            dma((ROUNDS, PLANE)),
        ],
        compiler_params=pltpu.CompilerParams(
            collective_id=0, has_side_effects=True, vmem_limit_bytes=60 * 1024 * 1024
        ),
    )(
        jnp.transpose(thickness, (1, 0, 2)),
        jnp.transpose(tracer_mass, (1, 0, 2)),
        jnp.transpose(zonal_courant, (1, 0, 2)),
        jnp.transpose(merid_courant, (1, 0, 2)),
        cutoffs.reshape(-1, lat_rows),
        *tables,
    )
    return tuple(jnp.transpose(out, (1, 0, 2)) for out in outs)


def solution(mesh):
    placed = P(None, "lon", "lat")
    return jax.shard_map(
        on_device,
        mesh=mesh,
        in_specs=(placed, placed, placed, placed, P()),
        out_specs=(placed, placed),
        check_vma=False,
    )
```

```python
import functools

import jax
import jax.numpy as jnp
import ml_dtypes
import numpy as np
from jax import lax
from jax.experimental import pallas as pl
from jax.experimental.pallas import tpu as pltpu
from jax.sharding import PartitionSpec as P

KW = 256
SUBSTEPS = 2
PLANE = 8
ROUNDS = 4
CHIPS = PLANE // 2
MESH = pl.DeviceIdType.MESH


def split_table(table):
    high = table.astype(ml_dtypes.bfloat16)
    low = (table - high.astype(np.float64)).astype(ml_dtypes.bfloat16)
    return high, low


def dft_tables(columns, padded, inverse_rows):
    points = columns * PLANE * 2
    longitude = np.arange(PLANE * columns).reshape(PLANE, columns, 1)
    angle = (longitude * np.arange(KW) % points) * (2.0 * np.pi / points)
    table = np.concatenate([np.cos(angle), np.sin(angle)], axis=2)
    forward = np.zeros((PLANE, padded, 2 * KW))
    forward[:, :columns] = table
    inverse = np.zeros((PLANE, inverse_rows, 2 * KW))
    inverse[:, :columns] = table
    forward = forward.reshape(PLANE * padded, 2 * KW).T.copy()
    return split_table(forward) + split_table(inverse.reshape(PLANE * inverse_rows, 2 * KW))


def halves(value):
    high = value.astype(jnp.bfloat16)
    return high, (value - high.astype(jnp.float32)).astype(jnp.bfloat16)


def dot(left, right):
    return jnp.dot(left, right, preferred_element_type=jnp.float32)


def product(left_high, left_low, right):
    right_high, right_low = halves(right)
    return dot(left_high, right_high) + dot(left_high, right_low) + dot(left_low, right_high)


def kernel(
    columns, padded, inverse_rows,
    thick_in, tracer_in, zonal_in, merid_in, cuts, fwd_hi_in, fwd_lo_in, inv_hi_in, inv_lo_in,
    out,
    fwd_hi, fwd_lo, inv_hi, inv_lo, table_sem,
    field, zonal, merid, adv, circle, back, passed, spec, spec_in, halo, edge, edge_in, rim, rim_in,
    in_sem, out_sem, halo_send, edge_recv, rim_recv, mig_send, mig_recv, fwd_send, fwd_recv,
    swap_send, swap_recv, ret_send, ret_recv, home_send, home_recv,
):
    band = lax.axis_index("lat")
    lon = lax.axis_index("lon")
    mine = lon % PLANE
    plane = lon - mine
    chip = mine // 2
    across = (lon + PLANE) % (2 * PLANE)
    east = (lon + 1) % (2 * PLANE)
    west = (lon + 2 * PLANE - 1) % (2 * PLANE)
    last_band = band // 7
    first_band = 1 - (band + 7) // 8
    helper_x = (band // 4) * 4 + 3 - band % 4
    helper_z = (band + 4) % 8
    polar = (band < 2) | (band >= 6)
    helping = jnp.logical_not(polar)

    def loop(count, body):
        def run(index, carry):
            body(index)
            return carry

        lax.fori_loop(0, count, run, 0)

    def inner(ref, *place):
        return ref.at[place + (pl.ds(0, columns),)]

    def load_copies(group, level):
        height = group * PLANE + level
        half, slab = level // CHIPS, 2 * (level % CHIPS)
        return [
            pltpu.make_async_copy(thick_in.at[:, height], inner(field, half, group, slab), in_sem.at[group, level, 0]),
            pltpu.make_async_copy(tracer_in.at[:, height], inner(field, half, group, slab + 1), in_sem.at[group, level, 1]),
            pltpu.make_async_copy(zonal_in.at[:, height], inner(zonal, group, level), in_sem.at[group, level, 2]),
            pltpu.make_async_copy(merid_in.at[:, height], inner(merid, group, level), in_sem.at[group, level, 3]),
        ]

    def store_copies(group, level):
        height = group * PLANE + level
        half, slab = level // CHIPS, 2 * (level % CHIPS)
        return [
            pltpu.make_async_copy(inner(field, half, group, slab), out.at[0, :, height], out_sem.at[group, level, 0]),
            pltpu.make_async_copy(inner(field, half, group, slab + 1), out.at[1, :, height], out_sem.at[group, level, 1]),
        ]

    def load(index):
        for copy in load_copies(index // PLANE, index % PLANE):
            copy.start()

    loop(ROUNDS * PLANE, load)
    tables = [
        pltpu.make_async_copy(fwd_hi_in, fwd_hi, table_sem.at[0]),
        pltpu.make_async_copy(fwd_lo_in, fwd_lo, table_sem.at[1]),
        pltpu.make_async_copy(inv_hi_in, inv_hi, table_sem.at[2]),
        pltpu.make_async_copy(inv_lo_in, inv_lo, table_sem.at[3]),
    ]
    for table in tables:
        table.start()

    barrier = pltpu.get_barrier_semaphore()
    partners = [(band, plane + (mine + step) % PLANE) for step in range(1, PLANE)]
    partners += [(band, across), (band, east), (band, west)]
    partners += [((band + 1) % 8, lon), ((band + 7) % 8, lon), (helper_x, lon), (helper_z, across)]
    for partner in partners:
        pl.semaphore_signal(barrier, inc=1, device_id=partner, device_id_type=MESH)

    row = lax.broadcasted_iota(jnp.int32, (padded, 128), 0)
    lane = lax.broadcasted_iota(jnp.int32, (padded, 128), 1)
    rest = pl.ds(columns, padded - columns)
    blank = jnp.zeros((padded - columns, 128), jnp.float32)

    def clear(index):
        group, level = index // PLANE, index % PLANE
        field[0, group, level, rest] = blank
        field[1, group, level, rest] = blank
        zonal[group, level, rest] = blank
        circle[group, level, rest] = blank
        merid[group, level, rest] = blank

    loop(ROUNDS * PLANE, clear)
    pl.semaphore_wait(barrier, len(partners))

    def remote(src, dst, send, recv, device):
        return pltpu.make_async_remote_copy(
            src_ref=src, dst_ref=dst, send_sem=send, recv_sem=recv, device_id=device, device_id_type=MESH
        )

    def halo_copies(step, group):
        return [
            remote(rim.at[step, group, 1], rim_in.at[step, group, 0], halo_send.at[step, group, 0],
                   rim_recv.at[step, group, 0], (band, east)),
            remote(rim.at[step, group, 0], rim_in.at[step, group, 1], halo_send.at[step, group, 1],
                   rim_recv.at[step, group, 1], (band, west)),
            remote(edge.at[step, group, pl.ds(64, 3 * PLANE)], edge_in.at[step, group, last_band], halo_send.at[step, group, 2],
                   edge_recv.at[step, group, last_band],
                   (band + 1 - last_band, (lon + PLANE * last_band) % (2 * PLANE))),
            remote(edge.at[step, group, pl.ds(0, 3 * PLANE)], edge_in.at[step, group, 1 - first_band], halo_send.at[step, group, 3],
                   edge_recv.at[step, group, 1 - first_band],
                   (band - 1 + first_band, (lon + PLANE * first_band) % (2 * PLANE))),
        ]

    def halo_wait(step, group):
        for side in range(2):
            remote(rim.at[step, group, 0], rim_in.at[step, group, side], halo_send.at[step, group, 0],
                   rim_recv.at[step, group, side], (band, east)).wait_recv()
            remote(edge.at[step, group, pl.ds(0, 3 * PLANE)], edge_in.at[step, group, side], halo_send.at[step, group, 0],
                   edge_recv.at[step, group, side], (band, across)).wait_recv()

    def pack(step, group):
        def one(level, packed):
            half, slab = level // CHIPS, 2 * (level % CHIPS)
            values = [field[half, group, slab], field[half, group, slab + 1], merid[group, level]]
            for array, value in enumerate(values):
                place = array * PLANE + level
                packed = jnp.where(lane == place, pltpu.roll(value, place, 1), packed)
                packed = jnp.where(lane == 64 + place, pltpu.roll(value, 65 + place, 1), packed)
            outer = [field.at[half, group, slab], field.at[half, group, slab + 1], zonal.at[group, level]]
            for array, ref in enumerate(outer):
                place = array * PLANE + level
                rim[step, group, 0, pl.ds(place, 1)] = ref[pl.ds(0, 1)]
                rim[step, group, 1, pl.ds(place, 1)] = ref[pl.ds(columns - 1, 1)]
            return packed

        packed = lax.fori_loop(0, PLANE, one, jnp.zeros((padded, 128), jnp.float32))
        edge[step, group] = jnp.transpose(packed)
        for copy in halo_copies(step, group):
            copy.start()

    sign_south = 1.0 - 2.0 * first_band.astype(jnp.float32)
    sign_north = 1.0 - 2.0 * last_band.astype(jnp.float32)

    def advect(step, group, level):
        half, slab = level // CHIPS, 2 * (level % CHIPS)

        def eastward(value, rim_row):
            return jnp.where(row == columns - 1, rim_row, pltpu.roll(value, padded - 1, 0))

        def rims(place):
            return rim_in[step, group, 0, pl.ds(place, 1)], rim_in[step, group, 1, pl.ds(place, 1)]

        def northward(place, value, sign):
            column = pltpu.roll(halo[1], 127 - place, 1)
            return jnp.where(lane == 127, column if sign is None else sign * column, pltpu.roll(value, 127, 1))

        def southward(place, value, sign):
            column = pltpu.roll(halo[0], 128 - place, 1)
            return jnp.where(lane == 0, column if sign is None else sign * column, pltpu.roll(value, 1, 1))

        a = zonal[group, level]
        m = merid[group, level]
        west_a, east_a = rims(2 * PLANE + level)
        face_east = 0.5 * (a + eastward(a, east_a))
        face_west = 0.5 * (west_a + a[0:1])
        face_north = 0.5 * (m + northward(2 * PLANE + level, m, sign_north))
        face_south = 0.5 * (southward(2 * PLANE + level, m, sign_south) + m)
        results = []
        for array in range(2):
            f = field[half, group, slab + array]
            place = array * PLANE + level
            west_f, east_f = rims(place)
            flux_east = jnp.maximum(face_east, 0.0) * f + jnp.minimum(face_east, 0.0) * eastward(f, east_f)
            first_west = jnp.maximum(face_west, 0.0) * west_f + jnp.minimum(face_west, 0.0) * f[0:1]
            flux_west = jnp.where(row == 0, first_west, pltpu.roll(flux_east, 1, 0))
            flux_north = jnp.maximum(face_north, 0.0) * f + jnp.minimum(face_north, 0.0) * northward(place, f, None)
            flux_south = jnp.maximum(face_south, 0.0) * southward(place, f, None) + jnp.minimum(face_south, 0.0) * f
            result = f - (flux_east - flux_west) - (flux_north - flux_south)
            results.append(jnp.where(row < columns, result, 0.0))
        return results


    rows = pl.ds(0, columns)

    def mig_copy(unit, place, device):
        pair = pl.ds(2 * place, 2)
        return remote(adv.at[1, unit, pair, rows], adv.at[0, unit, pair, rows], mig_send.at[unit, place], mig_recv.at[unit, place],
                      device)

    def fwd_copy(unit, slab):
        return remote(adv.at[0, unit, slab, rows], circle.at[unit, mine, rows], fwd_send.at[unit, slab], fwd_recv.at[unit, mine],
                      (band, plane + slab))

    def own_copy(unit):
        return pltpu.make_async_copy(adv.at[0, unit, mine, rows], circle.at[unit, mine, rows], fwd_send.at[unit, mine])

    def swap_copy(step, unit):
        return remote(spec.at[unit], spec_in.at[step, unit], swap_send.at[unit], swap_recv.at[unit], (band, across))

    def ret_copy(unit, other, target):
        return remote(back.at[unit, other, rows], target.at[unit, mine, rows], ret_send.at[unit, other], ret_recv.at[unit, mine],
                      (band, plane + other))

    def home_copy(unit, slab, device):
        return remote(passed.at[unit, slab, rows], field.at[1, unit, slab, rows], home_send.at[unit, slab], home_recv.at[unit, slab],
                      device)

    def send_forward(unit, slab):
        @pl.when(slab != mine)
        def _():
            fwd_copy(unit, slab).start()

        @pl.when(slab == mine)
        def _():
            own_copy(unit).start()

    def given(unit):
        def one(index):
            ret_copy(unit, (mine + 1 + index) % PLANE, passed).wait_send()

        loop(PLANE - 1, one)

    def handed(unit):
        def one(slab):
            home_copy(unit, slab, (helper_x, lon)).wait_send()

        given(unit)
        loop(PLANE, one)

    def prepare(item):
        step, unit = item // ROUNDS, item % ROUNDS

        @pl.when(step == 0)
        def _():
            def loaded(level):
                for copy in load_copies(unit, level):
                    copy.wait()

            loop(PLANE, loaded)

        @pl.when((step > 0) & polar)
        def _():
            def landed(index):
                source = (mine + PLANE - 1 - index) % PLANE
                remote(back.at[unit, source, rows], field.at[0, unit, source, rows], ret_send.at[unit, source],
                       ret_recv.at[unit, source], (band, plane + source)).wait_recv()

            def sent(place):
                mig_copy(unit, place, (helper_x, lon)).wait_send()

            def home(slab):
                home_copy(unit, slab, (helper_x, lon)).wait_recv()

            given(unit)
            loop(PLANE - 1, landed)
            loop(CHIPS, sent)
            loop(PLANE, home)

        @pl.when(step < SUBSTEPS)
        def _():
            pack(step, unit)

        @pl.when(step == SUBSTEPS)
        def _():
            def store(level):
                for copy in store_copies(unit, level):
                    copy.start()

            loop(PLANE, store)

    def advance(item):
        step, unit = item // ROUNDS, item % ROUNDS
        halo_wait(step, unit)
        unused = jnp.zeros((128 - 3 * PLANE, padded), jnp.float32)
        for side in range(2):
            halo[side] = jnp.transpose(jnp.concatenate([edge_in[step, unit, side], unused], axis=0))

        def one(index):
            half = 1 - index % 2
            place = (chip + 1 + index // 2) % CHIPS
            slab = 2 * place
            first, second = advect(step, unit, half * CHIPS + place)

            @pl.when(helping)
            def _():
                field[half, unit, slab] = first
                field[half, unit, slab + 1] = second

            @pl.when(polar)
            def _():
                adv[half, unit, slab] = first
                adv[half, unit, slab + 1] = second

                @pl.when((half == 1) & (place < CHIPS // 2))
                def _():
                    mig_copy(unit, place, (helper_x, lon)).start()

                @pl.when((half == 1) & (place >= CHIPS // 2))
                def _():
                    mig_copy(unit, place, (helper_z, across)).start()

                @pl.when(half == 0)
                def _():
                    send_forward(unit, slab)
                    send_forward(unit, slab + 1)

        loop(PLANE, one)

    def relay(item):
        unit = item % ROUNDS

        @pl.when(item >= ROUNDS)
        def _():
            handed(unit)

        def one(index):
            place = (chip + 1 + index) % CHIPS
            mig_copy(unit, place, (helper_x, lon)).wait_recv()
            send_forward(unit, 2 * place)
            send_forward(unit, 2 * place + 1)

        loop(CHIPS, one)

    def transform(item):
        step, unit = item // ROUNDS, item % ROUNDS
        @pl.when(item == 0)
        def _():
            for table in tables:
                table.wait()

        own_copy(unit).wait()

        def arrived(index):
            source = (mine + PLANE - 1 - index) % PLANE
            remote(adv.at[0, unit, source, rows], circle.at[unit, source, rows], fwd_send.at[unit, source],
                   fwd_recv.at[unit, source], (band, plane + source)).wait_recv()

        loop(PLANE - 1, arrived)
        spec[unit] = product(fwd_hi[...], fwd_lo[...], circle[unit].reshape(PLANE * padded, 128))
        swap_copy(step, unit).start()

    wave_row = lax.broadcasted_iota(jnp.int32, (2 * KW, 128), 0)
    parity = 1.0 - 2.0 * (wave_row % 2).astype(jnp.float32)
    wave = wave_row % KW
    wave_weight = jnp.where(wave == 0, 1.0 / (2 * PLANE * columns), 2.0 / (2 * PLANE * columns))
    source_band = jnp.where(polar, band, jnp.where(mine < CHIPS, helper_x, helper_z))

    def restore(item):
        step, unit = item // ROUNDS, item % ROUNDS

        def sent(index):
            fwd_copy(unit, (mine + 1 + index) % PLANE).wait_send()

        loop(PLANE - 1, sent)
        swap_copy(step, unit).wait()
        kept = jnp.where(wave < cuts[pl.ds(source_band % 4, 1)], wave_weight, 0.0)
        kept_hi, kept_lo = halves((spec[unit] + parity * spec_in[step, unit]) * kept)

        def give(index):
            other = (mine + 1 + index) % PLANE
            place = pl.ds(pl.multiple_of(other * inverse_rows, inverse_rows), inverse_rows)
            value = dot(inv_hi[place], kept_hi) + dot(inv_hi[place], kept_lo) + dot(inv_lo[place], kept_hi)
            value = value[:padded]

            @pl.when(other != mine)
            def _():
                back[unit, other] = value

            @pl.when((other != mine) & polar)
            def _():
                ret_copy(unit, other, field.at[0]).start()

            @pl.when((other != mine) & helping)
            def _():
                ret_copy(unit, other, passed).start()

            @pl.when((other == mine) & polar)
            def _():
                field[0, unit, mine] = value

            @pl.when((other == mine) & helping)
            def _():
                passed[unit, mine] = value

        loop(PLANE, give)

    def send_home(item):
        unit = item % ROUNDS

        def one(index):
            slab = (mine + PLANE - index) % PLANE

            @pl.when(slab != mine)
            def _():
                remote(back.at[unit, slab, rows], passed.at[unit, slab, rows], ret_send.at[unit, slab],
                       ret_recv.at[unit, slab], (band, plane + slab)).wait_recv()

            @pl.when(slab < CHIPS)
            def _():
                home_copy(unit, slab, (helper_x, lon)).start()

            @pl.when(slab >= CHIPS)
            def _():
                home_copy(unit, slab, (helper_z, across)).start()

        loop(PLANE, one)

    items = SUBSTEPS * ROUNDS

    def tick(time):
        @pl.when((time < items) & polar)
        def _():
            advance(time)

        @pl.when((time + 2 < ROUNDS) & polar)
        def _():
            prepare(time + 2)

        @pl.when((time + 1 >= ROUNDS) & (time < items) & polar)
        def _():
            prepare(time + 1)

        @pl.when((time >= 3) & helping)
        def _():
            send_home(time - 3)

        @pl.when((time >= 2) & (time < items + 2))
        def _():
            restore(time - 2)

        @pl.when((time >= 1) & (time < items + 1))
        def _():
            transform(time - 1)

        @pl.when((time >= items) & polar)
        def _():
            prepare(time + 1)

        @pl.when((time < items) & helping)
        def _():
            relay(time)
            advance(time)

        @pl.when((time < items) & helping)
        def _():
            prepare(time + ROUNDS)

    @pl.when(polar)
    def _():
        loop(2, prepare)

    @pl.when(helping)
    def _():
        loop(ROUNDS, prepare)

    loop(items + 3, tick)

    @pl.when(helping)
    def _():
        loop(ROUNDS, handed)

    def halo_done(index):
        for copy in halo_copies(index // ROUNDS, index % ROUNDS):
            copy.wait_send()

    loop(items, halo_done)

    def stored(index):
        for copy in store_copies(index // PLANE, index % PLANE):
            copy.wait()

    loop(ROUNDS * PLANE, stored)


def on_device(thickness, tracer_mass, zonal_courant, merid_courant, cutoffs):
    levels, columns, lat_rows = thickness.shape
    padded = -(-columns // 8) * 8
    inverse_rows = -(-columns // 16) * 16
    tables = [jnp.asarray(table) for table in dft_tables(columns, padded, inverse_rows)]
    shape = (columns, levels, lat_rows)
    f32 = jnp.float32
    dma = pltpu.SemaphoreType.DMA
    piece = (PLANE, padded, 128)
    outs = pl.pallas_call(
        functools.partial(kernel, columns, padded, inverse_rows),
        out_shape=jax.ShapeDtypeStruct((2,) + shape, f32),
        in_specs=[pl.BlockSpec(memory_space=pl.ANY)] * 4
        + [pl.BlockSpec(memory_space=pltpu.VMEM)]
        + [pl.BlockSpec(memory_space=pl.ANY)] * 4,
        out_specs=pl.BlockSpec(memory_space=pl.ANY),
        scratch_shapes=[pltpu.VMEM(table.shape, table.dtype) for table in tables]
        + [
            dma((4,)),
            pltpu.VMEM((2, ROUNDS) + piece, f32),
            pltpu.VMEM((ROUNDS,) + piece, f32),
            pltpu.VMEM((ROUNDS,) + piece, f32),
            pltpu.VMEM((2, ROUNDS) + piece, f32),
            pltpu.VMEM((ROUNDS,) + piece, f32),
            pltpu.VMEM((ROUNDS,) + piece, f32),
            pltpu.VMEM((ROUNDS,) + piece, f32),
            pltpu.VMEM((ROUNDS, 2 * KW, 128), f32),
            pltpu.VMEM((SUBSTEPS, ROUNDS, 2 * KW, 128), f32),
            pltpu.VMEM((2, padded, 128), f32),
            pltpu.VMEM((SUBSTEPS, ROUNDS, 128, padded), f32),
            pltpu.VMEM((SUBSTEPS, ROUNDS, 2, 3 * PLANE, padded), f32),
            pltpu.VMEM((SUBSTEPS, ROUNDS, 2, 3 * PLANE, 128), f32),
            pltpu.VMEM((SUBSTEPS, ROUNDS, 2, 3 * PLANE, 128), f32),
            dma((ROUNDS, PLANE, 4)),
            dma((ROUNDS, PLANE, 2)),
            dma((SUBSTEPS, ROUNDS, 4)),
            dma((SUBSTEPS, ROUNDS, 2)),
            dma((SUBSTEPS, ROUNDS, 2)),
            dma((ROUNDS, CHIPS)),
            dma((ROUNDS, CHIPS)),
            dma((ROUNDS, PLANE)),
            dma((ROUNDS, PLANE)),
            dma((ROUNDS,)),
            dma((ROUNDS,)),
            dma((ROUNDS, PLANE)),
            dma((ROUNDS, PLANE)),
            dma((ROUNDS, PLANE)),
            dma((ROUNDS, PLANE)),
        ],
        compiler_params=pltpu.CompilerParams(
            collective_id=0, has_side_effects=True, vmem_limit_bytes=60 * 1024 * 1024
        ),
    )(
        jnp.transpose(thickness, (1, 0, 2)),
        jnp.transpose(tracer_mass, (1, 0, 2)),
        jnp.transpose(zonal_courant, (1, 0, 2)),
        jnp.transpose(merid_courant, (1, 0, 2)),
        cutoffs.reshape(-1, lat_rows),
        *tables,
    )
    return tuple(jnp.transpose(out, (1, 0, 2)) for out in outs)


def solution(mesh):
    placed = P(None, "lon", "lat")
    return jax.shard_map(
        on_device,
        mesh=mesh,
        in_specs=(placed, placed, placed, placed, P()),
        out_specs=(placed, placed),
        check_vma=False,
    )
```
